256 devices in a mesh: section: 64 (over z_hi, y, x, core), tensor: 4 (over z_lo).
Axes of the slice: x: 4, y: 4, z: 8 (z_hi: 2, z_lo: 4; z = z_hi * 4 + z_lo), core: 2. Of those that a mesh axis runs over, the one named last changes fastest.
Arguments:
- stash: bfloat16 [64, 8, 6144], P('section', None, 'tensor'), may hold values from -6 to 6
- out_grad: bfloat16 [64, 8, 6144], P('section', None, 'tensor'), may hold values from -6 to 6
- router_weight: bfloat16 [4, 6144], P(None, 'tensor'), may hold values from -0.078125 to 0.078125
- gate_weight: bfloat16 [32768, 6144], P('section', 'tensor'), may hold values from -0.078125 to 0.078125
- up_weight: bfloat16 [32768, 6144], P('section', 'tensor'), may hold values from -0.078125 to 0.078125
- down_weight: bfloat16 [32768, 6144], P('section', 'tensor'), may hold values from -0.0625 to 0.0625
- expert_ids: int32 [64, 8, 2], P('section'), may hold values from 0 to 3, all different within a row; in each aligned block of 8 rows (0 to 7, 8 to 15, ..., all dimensions but the last counted through in order) at most 5 rows name the same one
Outputs:
- in_grad: bfloat16 [64, 8, 6144], P('section', None, 'tensor')
- gate_grad: bfloat16 [32768, 6144], P('section', 'tensor')
- up_grad: bfloat16 [32768, 6144], P('section', 'tensor')
- down_grad: bfloat16 [32768, 6144], P('section', 'tensor')
- router_grad: float32 [4, 6144], P(None, 'tensor')
- aux_losses: float32 [64, 2], P('section')
The draws below stay inside these ranges and needn't reach their ends.
Inputs may be any that keep to these rules, and one draw needn't show every extreme that they name: `expert_ids`: each token names two different experts; among the 8 tokens of one block no expert is named more than 5 times, a bound that some block reaches.
All inputs are finite; a program needn't handle non-finite values.
Results may differ from the reference program's by a relative error of at most 0.0049.
Values may be sent and summed in bfloat16 or wider, within the bound.
No kernel may reach another device: no remote copies, remote signals or barrier semaphores. Data moves between devices by JAX's collectives and lax.ppermute only.
A program may use at most 64 MiB of HBM per device.

```python
import math
import jax
import jax.numpy as jnp
import numpy as np
from jax import lax

D = 6144
EXPERTS = 4
TOK = 8
HID_ALL = 8192
CAP = 5
SECTIONS = 64


def block_levels(rng, dims, cuts, low, top_value):
    level, own = 1.0, jax.random.fold_in(rng, 6)
    for dim, parts in cuts:
        heights = jnp.exp(jax.random.uniform(jax.random.fold_in(own, dim), (parts,), jnp.float32, low / len(cuts), top_value / len(cuts)))
        level = level * jnp.repeat(heights, dims[dim] // parts).reshape([-1 if axis == dim else 1 for axis in range(len(dims))])
    return level


def deal_out(key, own, number, rows, number_of, top, reach, skew):
    ranking = jax.random.permutation(key, number_of)
    packed, usual = portions_of(number_of, rows * top, reach, skew, True), portions_of(number_of, rows * top, reach, skew, False)
    places = jnp.arange(number_of)

    def named(lengths, turn):
        used = int((lengths > 0).sum())
        fixed = max(1, used // 4)
        moved = fixed + (places - fixed + turn * (used - fixed)) % max(1, number_of - fixed)
        return jnp.zeros((number_of,), jnp.int32).at[ranking[jnp.where(places < fixed, places, moved)]].set(jnp.asarray(lengths, jnp.int32))

    lengths = jnp.where(number % 4 == 0, named(packed, number // 4), named(usual, number - number // 4 - 1))
    mixed = jax.random.permutation(jax.random.fold_in(own, 3), number_of)
    source_of, taker = mixed[0:number_of // 2 * 2:2], mixed[1:number_of // 2 * 2:2]
    room = jnp.minimum(lengths[source_of] - 1, reach - lengths[taker]) // 2
    room = jnp.where((source_of == ranking[0]) | (taker == ranking[0]) | (lengths[taker] == 0), 0, jnp.maximum(room, 0))
    moved = jax.random.randint(jax.random.fold_in(own, 4), (number_of // 2,), 0, 1 << 20) % (room + 1)
    lengths = lengths.at[source_of].add(-moved).at[taker].add(moved)
    members = jnp.searchsorted(jnp.cumsum(lengths), jnp.arange(rows * top), side="right").astype(jnp.int32)
    table = members.reshape(top, rows).T
    table = table[jax.random.permutation(jax.random.fold_in(own, 1), rows)]
    turn = jax.random.randint(jax.random.fold_in(own, 2), (rows, 1), 0, top)
    return jnp.take_along_axis(table, (jnp.arange(top)[None, :] + turn) % top, axis=1)


def portions_of(count, total, limit, lean, full):
    weights = [(1 << 20) // math.isqrt(grade ** lean) + 1 for grade in range(1, count + 1)]
    largest = limit if full else min(limit, max(-(-total // count), total * weights[0] // sum(weights)))
    least = 1 if total - largest >= count - 1 else 0
    holding, surplus = [largest] + [least] * (count - 1), total - largest - least * (count - 1)
    while surplus > 0:
        free = [i for i in range(1, count) if holding[i] < largest] or [i for i in range(1, count) if holding[i] < limit]
        pool, left = sum([weights[i] for i in free]), surplus
        for i in free:
            more = min(limit - holding[i], max(1, left * weights[i] // pool), surplus)
            holding[i] = holding[i] + more
            surplus = surplus - more
    return np.array(holding)


def bell_draw(own_key, extent, deviation, bound, shards=(), held_as=jnp.bfloat16):
    loudness = block_levels(own_key, extent, shards, -0.22, 0.18) if shards else 1.0
    entries = jax.random.normal(own_key, extent, jnp.float32) * deviation * loudness
    return jnp.minimum(jnp.maximum(entries, -bound), bound).astype(held_as)


def setup_inputs(seed: int = 0) -> dict:
    streams_of = jax.random.split(jax.random.key(seed), 8)
    stash = bell_draw(streams_of[0], (SECTIONS, TOK, D), 1.0, 6.0, ((0, 64), (2, 4)))
    out_grad = bell_draw(streams_of[1], (SECTIONS, TOK, D), 1.0, 6.0, ((0, 64), (2, 4)))
    router_weight = bell_draw(streams_of[2], (EXPERTS, D), D ** -0.5, 0.078125, ((1, 4),))
    gate_weight = bell_draw(streams_of[3], (EXPERTS * HID_ALL, D), D ** -0.5, 0.078125, ((0, 64), (1, 4)))
    up_weight = bell_draw(streams_of[4], (EXPERTS * HID_ALL, D), D ** -0.5, 0.078125, ((0, 64), (1, 4)))
    down_weight = bell_draw(streams_of[5], (EXPERTS * HID_ALL, D), HID_ALL ** -0.5, 0.0625, ((0, 64), (1, 4)))
    expert_ids_keys = jax.random.split(jax.random.fold_in(streams_of[6], 1), SECTIONS * TOK // TOK)
    expert_ids_turns = jax.random.permutation(jax.random.fold_in(streams_of[6], 3), SECTIONS * TOK // TOK)
    expert_ids = jax.vmap(lambda own, number: deal_out(jax.random.fold_in(streams_of[6], 2), own, number, TOK, EXPERTS, 2, CAP, 2))(expert_ids_keys, expert_ids_turns).reshape((SECTIONS, TOK, 2))
    return {"stash": stash, "out_grad": out_grad, "router_weight": router_weight, "gate_weight": gate_weight, "up_weight": up_weight, "down_weight": down_weight, "expert_ids": expert_ids}


Z_WEIGHT = 0.25
BALANCE_WEIGHT = 1.0


def block_routes(chosen_blocks, experts, capacity):
    blocks = chosen_blocks.shape[0]
    flat_ids = chosen_blocks.reshape(blocks, -1)
    labels = jnp.arange(experts, dtype=jnp.int32)
    onehot = (flat_ids[:, :, None] == labels[None, None, :]).astype(jnp.int32)
    before = (jnp.cumsum(onehot, axis=1) - onehot).astype(jnp.int32)
    position = jnp.sum(before * onehot, axis=2).astype(jnp.int32)
    block_number = jnp.arange(blocks, dtype=jnp.int32)[:, None]
    slot_of = (flat_ids * (blocks * capacity) + block_number * capacity + position).astype(jnp.int32)
    pair_count = flat_ids.shape[0] * flat_ids.shape[1]
    source = jnp.full((experts * blocks * capacity,), pair_count, dtype=jnp.int32)
    source = source.at[slot_of.reshape(-1)].set(jnp.arange(pair_count, dtype=jnp.int32))
    filled = source < pair_count
    clipped = jnp.minimum(source, pair_count - 1).astype(jnp.int32)
    counts = jnp.sum(onehot, axis=1).astype(jnp.int32)
    return slot_of, clipped, filled, counts


def pair_gates(logits, chosen):
    picked = jnp.take_along_axis(logits, chosen, axis=1)
    return jax.nn.sigmoid(picked[:, 0] - picked[:, 1])


def router_terms(logits, chosen, counts, lead_gate, dgate_pairs):
    tokens, experts = logits.shape
    exp_logits = jnp.exp(logits)
    exp_total = jnp.sum(exp_logits, axis=1, keepdims=True)
    log_total = jnp.log(exp_total)
    prob_rows = exp_logits / exp_total
    fraction = counts.astype(jnp.float32) / (2.0 * tokens)
    labels = jnp.arange(experts, dtype=jnp.int32)[None, :]
    toward = (chosen[:, 0:1] == labels).astype(jnp.float32) - (chosen[:, 1:2] == labels).astype(jnp.float32)
    spread = lead_gate * (1.0 - lead_gate) * (dgate_pairs[:, 0] - dgate_pairs[:, 1])
    balance_pull = BALANCE_WEIGHT * experts * fraction[None, :]
    local_part = 2.0 * Z_WEIGHT * log_total * prob_rows + prob_rows * (balance_pull - jnp.sum(prob_rows * balance_pull, axis=1, keepdims=True))
    dlogits = spread[:, None] * toward + local_part
    losses = jnp.stack([jnp.mean(log_total[:, 0] * log_total[:, 0]), experts * jnp.sum(fraction * jnp.mean(prob_rows, axis=0))])
    return dlogits, losses


def reference(stash, out_grad, router_weight, gate_weight, up_weight, down_weight, expert_ids):
    sections = stash.shape[0]
    token_count = stash.shape[1]
    model_width = stash.shape[2]
    experts = router_weight.shape[0]
    hidden = gate_weight.shape[0] // experts
    x_rows = stash[::-1].reshape(-1, model_width)
    g_rows = out_grad.reshape(-1, model_width)
    total_tokens = x_rows.shape[0]
    chosen = expert_ids.reshape(-1, 2)
    logits = jnp.dot(x_rows, router_weight.T, preferred_element_type=jnp.float32)
    lead_gate = pair_gates(logits, chosen)
    gate_pairs = jnp.stack([lead_gate, 1.0 - lead_gate], axis=1).reshape(-1)
    slot_of, clipped, filled, counts = block_routes(expert_ids, experts, CAP)
    slot_span = sections * CAP

    def one_expert(expert):
        start = (expert * slot_span).astype(jnp.int32)
        source = lax.dynamic_slice_in_dim(clipped, start, slot_span, 0)
        used = lax.dynamic_slice_in_dim(filled, start, slot_span, 0)
        row_index = (source // 2).astype(jnp.int32)
        keep = used[:, None]
        x_slot = jnp.where(keep, jnp.take(x_rows, row_index, axis=0), jnp.zeros((), x_rows.dtype))
        g_slot = jnp.where(keep, jnp.take(g_rows, row_index, axis=0), jnp.zeros((), g_rows.dtype))
        w_slot = jnp.where(used, jnp.take(gate_pairs, source), 0.0)[:, None]
        row_start = (expert * hidden).astype(jnp.int32)
        w_gate = lax.dynamic_slice_in_dim(gate_weight, row_start, hidden, 0)
        w_up = lax.dynamic_slice_in_dim(up_weight, row_start, hidden, 0)
        w_down = lax.dynamic_slice_in_dim(down_weight, row_start, hidden, 0)
        gate_proj = jnp.dot(x_slot, w_gate.T, preferred_element_type=jnp.float32)
        up_proj = jnp.dot(x_slot, w_up.T, preferred_element_type=jnp.float32)
        back_proj = jnp.dot(g_slot, w_down.T, preferred_element_type=jnp.float32)
        gate_sig = jax.nn.sigmoid(gate_proj)
        silu_gate = gate_proj * gate_sig
        dgate_slot = jnp.sum(silu_gate * up_proj * back_proj, axis=1)
        scaled = w_slot * back_proj
        d_gate_proj = (scaled * up_proj * gate_sig * (1.0 + gate_proj * (1.0 - gate_sig))).astype(jnp.bfloat16)
        d_up_proj = (scaled * silu_gate).astype(jnp.bfloat16)
        weighted_act = (w_slot * silu_gate * up_proj).astype(jnp.bfloat16)
        dx_slot = jnp.dot(d_gate_proj, w_gate, preferred_element_type=jnp.float32) + jnp.dot(d_up_proj, w_up, preferred_element_type=jnp.float32)
        dx_tokens = jnp.zeros((total_tokens, model_width), jnp.float32).at[row_index].add(jnp.where(keep, dx_slot, 0.0))
        grad_gate = jnp.dot(d_gate_proj.T, x_slot, preferred_element_type=jnp.float32).astype(jnp.bfloat16)
        grad_up = jnp.dot(d_up_proj.T, x_slot, preferred_element_type=jnp.float32).astype(jnp.bfloat16)
        grad_down = jnp.dot(weighted_act.T, g_slot, preferred_element_type=jnp.float32).astype(jnp.bfloat16)
        return dx_tokens, dgate_slot, grad_gate, grad_up, grad_down

    dx_all, dgate_all, grad_gate, grad_up, grad_down = lax.map(one_expert, jnp.arange(experts, dtype=jnp.int32))
    expert_dx = jnp.sum(dx_all, axis=0)
    dgate_pairs = jnp.take(dgate_all.reshape(-1), slot_of.reshape(-1)).reshape(sections, token_count, 2)
    dlogits, losses = jax.vmap(router_terms)(logits.reshape(sections, token_count, experts), expert_ids, counts, lead_gate.reshape(sections, token_count), dgate_pairs)
    dlogits = dlogits.reshape(total_tokens, experts)
    router_dx = jnp.dot(dlogits, router_weight.astype(jnp.float32), precision=lax.Precision.HIGHEST)
    in_grad = (g_rows.astype(jnp.float32) + expert_dx + router_dx).astype(jnp.bfloat16).reshape(sections, token_count, model_width)
    router_grad = jnp.dot(dlogits.T, x_rows.astype(jnp.float32), precision=lax.Precision.HIGHEST)
    shape_all = (experts * hidden, model_width)
    return (in_grad, grad_gate.reshape(shape_all), grad_up.reshape(shape_all), grad_down.reshape(shape_all), router_grad, losses)
```

```python
import jax
import jax.numpy as jnp
from jax import lax
from jax.sharding import Mesh, PartitionSpec as P

CAP = 5
Z_WEIGHT = 0.25
BALANCE_WEIGHT = 1.0
BF = jnp.bfloat16
F32 = jnp.float32
HIGH = lax.Precision.HIGHEST


def split_pair(value):
    high = lax.reduce_precision(value, 8, 7)
    return high.astype(BF), (value - high).astype(BF)


def spread_out(value, axis):
    count = lax.axis_size(axis)
    return lax.all_to_all(jnp.broadcast_to(value[None], (count, *value.shape)), axis, 0, 0)


def core_swap(value):
    return lax.ppermute(value, "c", [(0, 1), (1, 0)])


def block_slots(ids, expert):
    match = (ids[..., 0] == expert) | (ids[..., 1] == expert)
    counted = match.astype(jnp.int32)
    position = jnp.cumsum(counted, axis=-1) - counted
    return match, position


def shards(stash, out_grad, router_weight, gate_weight, up_weight, down_weight, expert_ids):
    e, q, c = lax.axis_index("e"), lax.axis_index("q"), lax.axis_index("c")
    experts, groups, cores = lax.axis_size("e"), lax.axis_size("q"), lax.axis_size("c")
    ways = lax.axis_size("t")
    tokens, width = stash.shape[1], stash.shape[2]
    hidden = gate_weight.shape[0]
    share = hidden // ways
    blocks = cores * groups * experts
    slots = blocks * CAP
    ids = expert_ids[0]
    x_here, g_own = stash[0], out_grad[0]

    id_columns = jnp.pad(ids.astype(BF), ((tokens, 0), (0, 126)))
    own = jnp.concatenate([jnp.concatenate([x_here, g_own], 0), id_columns], 1)
    first = spread_out(own, "e")
    x_quad = first[:, :tokens, :width].reshape(experts * tokens, width)
    g_quad = first[:, tokens:].reshape(experts * tokens, width + 128)
    x_near = spread_out(x_quad, "q").reshape(-1, width)
    g_near = spread_out(g_quad, "q").reshape(-1, width + 128)
    x_far, g_far = core_swap(x_near), core_swap(g_near)

    all_ids = jnp.concatenate([g_near[:, width : width + 2], g_far[:, width : width + 2]], 0)
    all_ids = all_ids.astype(jnp.int32).reshape(blocks, tokens, 2)
    match, position = block_slots(all_ids, e)
    slot = jnp.arange(blocks, dtype=jnp.int32)[:, None] * CAP + position
    slot = jnp.where(match, slot, -1)
    labels = jnp.arange(slots, dtype=jnp.int32)[None, :]
    pick_g = (slot.reshape(-1, 1) == labels).astype(BF)
    pick_x = (slot[::-1].reshape(-1, 1) == labels).astype(BF)
    half = blocks * tokens // 2

    def choose(pick, near, far):
        dims = (((0,), (0,)), ((), ()))
        picked = lax.dot_general(pick[:half], near, dims, preferred_element_type=F32)
        picked += lax.dot_general(pick[half:], far, dims, preferred_element_type=F32)
        return picked.astype(BF)

    x_slot = choose(pick_x, x_near, x_far)
    g_slot = choose(pick_g, g_near[:, :width], g_far[:, :width])
    expert_labels = jnp.arange(experts, dtype=jnp.int32)
    other = all_ids[..., 0] + all_ids[..., 1] - e
    toward_token = (expert_labels == e).astype(BF) - (
        other.reshape(-1, 1) == expert_labels
    ).astype(BF)
    toward = lax.dot_general(pick_g, toward_token, (((0,), (0,)), ((), ())), preferred_element_type=F32)
    used = jnp.sum(jnp.abs(toward), axis=1) > 0.5

    dims = (((1,), (1,)), ((), ()))
    gate_part = lax.dot_general(x_slot, gate_weight, dims, preferred_element_type=F32).astype(BF)
    up_part = lax.dot_general(x_slot, up_weight, dims, preferred_element_type=F32).astype(BF)
    back_part = lax.dot_general(g_slot, down_weight, dims, preferred_element_type=F32).astype(BF)
    slot_logits = lax.dot_general(x_slot, router_weight, dims, preferred_element_type=F32)
    lead_part = jnp.sum(slot_logits * toward, axis=1)
    x_far_blocks = x_far.reshape(groups, experts, tokens, width)
    x_own = lax.dynamic_slice(
        x_far_blocks, (groups - 1 - q, experts - 1 - e, 0, 0), (1, 1, tokens, width)
    )[0, 0]
    own_part = lax.dot_general(router_weight, x_own, dims, preferred_element_type=F32)
    notes = jnp.concatenate([lead_part, own_part.reshape(-1)])
    note_high, note_low = split_pair(notes)
    note_rows = jnp.pad(
        jnp.stack([note_high, note_low]), ((0, 14), (0, 3 * share - notes.shape[0]))
    )
    pieces = [
        jnp.concatenate(
            [
                jnp.concatenate(
                    [part[:, k * share : (k + 1) * share] for part in (gate_part, up_part, back_part)], 1
                ),
                note_rows,
            ],
            0,
        )
        for k in range(ways)
    ]
    summed = lax.all_to_all(jnp.stack(pieces), "t", 0, 0).astype(F32).sum(0)
    gate_proj, up_proj, back_proj = (
        summed[:slots, k * share : (k + 1) * share] for k in range(3)
    )
    notes = summed[slots] + summed[slots + 1]
    lead = notes[:slots]
    own_logits = notes[slots : slots + experts * tokens].reshape(experts, tokens).T
    w_slot = jnp.where(used, jax.nn.sigmoid(lead), 0.0)
    w_column = w_slot[:, None]

    gate_sig = jax.nn.sigmoid(gate_proj)
    silu_gate = gate_proj * gate_sig
    dgate_part = jnp.sum(silu_gate * up_proj * back_proj, axis=1)
    scaled = w_column * back_proj
    d_gate = (scaled * up_proj * gate_sig * (1.0 + gate_proj * (1.0 - gate_sig))).astype(BF)
    d_up = (scaled * silu_gate).astype(BF)
    weighted = (w_column * silu_gate * up_proj).astype(BF)
    dgate_high, dgate_low = split_pair(dgate_part)
    dgate_rows = jnp.pad(jnp.stack([dgate_high, dgate_low]), ((0, 14), (0, 3 * share - slots)))
    packed = jnp.concatenate([jnp.concatenate([d_gate, d_up, weighted], 1), dgate_rows], 0)
    whole = lax.all_gather(packed, "t", axis=0)
    d_gate, d_up, weighted = (
        whole[:, :slots, k * share : (k + 1) * share].transpose(1, 0, 2).reshape(slots, hidden)
        for k in range(3)
    )
    dgate = whole[:, slots : slots + 2, :slots].astype(F32).sum((0, 1))

    exp_logits = jnp.exp(own_logits)
    exp_total = jnp.sum(exp_logits, axis=1, keepdims=True)
    log_total = jnp.log(exp_total)
    prob_rows = exp_logits / exp_total
    counts = jnp.sum((ids.reshape(-1, 1) == expert_labels).astype(F32), axis=0)
    fraction = counts / (2.0 * tokens)
    balance_pull = BALANCE_WEIGHT * experts * fraction[None, :]
    local_part = 2.0 * Z_WEIGHT * log_total * prob_rows + prob_rows * (
        balance_pull - jnp.sum(prob_rows * balance_pull, axis=1, keepdims=True)
    )
    losses = jnp.stack(
        [
            jnp.mean(log_total[:, 0] * log_total[:, 0]),
            experts * jnp.sum(fraction * jnp.mean(prob_rows, axis=0)),
        ]
    )
    coefficient = (w_slot * (1.0 - w_slot) * dgate)[:, None] * toward
    router_part = jnp.dot(coefficient.T, x_slot.astype(F32), precision=HIGH) + jnp.dot(
        local_part.T, x_own.astype(F32), precision=HIGH
    )

    rw = router_weight.astype(F32)
    dx = (
        jnp.dot(d_gate, gate_weight, preferred_element_type=F32)
        + jnp.dot(d_up, up_weight, preferred_element_type=F32)
        + jnp.dot(coefficient, rw, precision=HIGH)
    )
    router_rows = jnp.concatenate(split_pair(router_part), 0)
    sent = jnp.concatenate([dx[slots // 2 :].astype(BF), router_rows], 0)
    got = core_swap(sent).astype(F32)
    pair_rows = (dx[: slots // 2] + got[: slots // 2]).astype(BF)
    got_router = got[slots // 2 : slots // 2 + experts] + got[slots // 2 + experts :]
    router_rows = jnp.concatenate(split_pair(router_part + got_router), 0)
    pair_rows = pair_rows.reshape(groups, experts * CAP, width)
    router_all = jnp.broadcast_to(router_rows[None], (groups, *router_rows.shape))
    sent = jnp.concatenate([pair_rows, router_all], 1)
    got = lax.all_to_all(sent, "q", 0, 0).astype(F32).sum(0)
    quad_rows = got[: experts * CAP].astype(BF).reshape(experts, CAP, width)
    router_part = got[experts * CAP : experts * CAP + experts] + got[experts * CAP + experts :]
    router_rows = jnp.concatenate(split_pair(router_part), 0)
    router_all = jnp.broadcast_to(router_rows[None], (experts, *router_rows.shape))
    padded = jnp.pad(quad_rows, ((0, 0), (0, 8 - CAP), (0, 0)))
    got = lax.all_to_all(jnp.concatenate([padded, router_all], 1), "e", 0, 0).astype(F32)
    router_grad = got[:, 8:].sum(0)
    router_grad = router_grad[:experts] + router_grad[experts:]

    own_match, own_position = block_slots(ids[None], expert_labels[:, None])
    where = jnp.where(own_match, own_position, -1)
    combine = (where[:, :, None] == jnp.arange(8, dtype=jnp.int32)).astype(F32)
    expert_dx = jnp.einsum("etk,ekd->td", combine, got[:, :8], precision=HIGH)
    router_dx = jnp.dot(local_part, rw, precision=HIGH)
    in_grad = (g_own.astype(F32) + expert_dx + router_dx).astype(BF)

    dims = (((0,), (0,)), ((), ()))
    gate_grad = lax.dot_general(d_gate, x_slot, dims, preferred_element_type=F32).astype(BF)
    up_grad = lax.dot_general(d_up, x_slot, dims, preferred_element_type=F32).astype(BF)
    down_grad = lax.dot_general(weighted, g_slot, dims, preferred_element_type=F32).astype(BF)
    return in_grad[None], gate_grad, up_grad, down_grad, router_grad, losses[None]


def solution(mesh):
    sections, ways = mesh.devices.shape
    experts, cores = 4, 2
    groups = sections // (experts * cores)
    fine = Mesh(mesh.devices.reshape(experts, groups, cores, ways), ("e", "q", "c", "t"))
    section = ("e", "q", "c")
    in_specs = (
        P(section, None, "t"),
        P(section, None, "t"),
        P(None, "t"),
        P(section, "t"),
        P(section, "t"),
        P(section, "t"),
        P(section, None, None),
    )
    out_specs = (
        P(section, None, "t"),
        P(section, "t"),
        P(section, "t"),
        P(section, "t"),
        P(None, "t"),
        P(section, None),
    )
    return jax.shard_map(shards, mesh=fine, in_specs=in_specs, out_specs=out_specs, check_vma=False)
```

```python
import functools

import jax
import jax.numpy as jnp
from jax import lax
from jax.experimental import pallas as pl
from jax.experimental.pallas import tpu as pltpu
from jax.sharding import Mesh, PartitionSpec as P

CAP = 5
Z_WEIGHT = 0.25
BALANCE_WEIGHT = 1.0
BF = jnp.bfloat16
F32 = jnp.float32
HIGH = lax.Precision.HIGHEST
PARTS = ((0, 3), (1, 2))
VMEM = pl.BlockSpec(memory_space=pltpu.VMEM)
SMEM = pl.BlockSpec(memory_space=pltpu.SMEM)
NT = (((1,), (1,)), ((), ()))
TN = (((0,), (0,)), ((), ()))


def matmul(a, b, dims=(((1,), (0,)), ((), ()))):
    return lax.dot_general(a, b, dims, preferred_element_type=F32)


def split_pair(value):
    high = value.astype(BF)
    return high, (value - high.astype(F32)).astype(BF)


def up_to(count, step):
    return -(-count // step) * step


def to_row(value):
    count = value.shape[0]
    padded = up_to(count, 128)
    if padded > count:
        value = jnp.concatenate([value, jnp.zeros((padded - count, 128), F32)], 0)
    return jnp.sum(value.T, axis=0, keepdims=True)


def to_column(row, count):
    padded = up_to(count, 128)
    return jnp.broadcast_to(row[:, :padded], (128, padded)).T[:count]


def project_kernel(
    chunks, width, share, has_own,
    place, near, far, gate_w, up_w, down_w, router_w,
    own, send1, send2, send3, x_slot, g_slot, toward, scatter, x_own, notes,
):
    e, q, t = place[0], place[1], place[2]
    e_value = e.astype(F32)
    rows = chunks * 16
    half = chunks * CAP
    row = lax.broadcasted_iota(jnp.int32, (rows, rows), 0)
    col = lax.broadcasted_iota(jnp.int32, (rows, rows), 1)
    earlier = ((row >> 4 == col >> 4) & (col < row)).astype(F32).astype(BF)
    mirror = (
        ((row >> 4) + (col >> 4) == chunks - 1) & ((row & 15) + 8 == (col & 15))
    ).astype(F32).astype(BF)
    compact = (
        (lax.broadcasted_iota(jnp.int32, (chunks * 8, rows), 0) >> 3
         == lax.broadcasted_iota(jnp.int32, (chunks * 8, rows), 1) >> 4)
        & ((lax.broadcasted_iota(jnp.int32, (chunks * 8, rows), 0) & 7) + 8
           == (lax.broadcasted_iota(jnp.int32, (chunks * 8, rows), 1) & 15))
    ).astype(F32).astype(BF)
    tall = lax.broadcasted_iota(jnp.int32, (rows, 128), 0)
    lane = lax.broadcasted_iota(jnp.int32, (rows, 128), 1).astype(F32)
    is_grad = (tall & 15) >= 8
    labels = lax.broadcasted_iota(jnp.int32, (rows, half), 1).astype(F32)

    def routes(block):
        ids = block[:, width:].astype(F32)
        first = jnp.broadcast_to(ids[:, 0:1], (rows, 128))
        second = jnp.broadcast_to(ids[:, 1:2], (rows, 128))
        match = is_grad & ((first == e_value) | (second == e_value))
        matched = match.astype(F32)
        position = matmul(earlier, matched.astype(BF))
        slot = jnp.where(match, (tall >> 4).astype(F32) * CAP + position, -1.0)
        pick = (jnp.broadcast_to(slot[:, 0:1], (rows, half)) == labels).astype(F32).astype(BF)
        other = first + second - e_value
        sign = matched * ((lane == e_value).astype(F32) - (lane == other).astype(F32))
        return pick, sign.astype(BF)

    pick_near, sign_near = routes(near)
    pick_far, sign_far = routes(far)
    mirror_near = matmul(mirror, pick_far).astype(BF)
    mirror_far = matmul(mirror, pick_near).astype(BF)
    x_slot[:half] = matmul(mirror_far, far[:, :width], TN).astype(BF)
    x_slot[half:] = matmul(mirror_near, near[:, :width], TN).astype(BF)
    g_slot[:half] = matmul(pick_near, near[:, :width], TN).astype(BF)
    g_slot[half:] = matmul(pick_far, far[:, :width], TN).astype(BF)
    toward[:half] = matmul(pick_near, sign_near, TN)
    toward[half:] = matmul(pick_far, sign_far, TN)
    scatter[: chunks * 8] = matmul(compact, pick_near).astype(BF)
    scatter[chunks * 8 :] = matmul(compact, pick_far).astype(BF)

    slots = 2 * half
    lead = to_row(matmul(x_slot[...], router_w[...], NT) * toward[...])
    notes[...] = jnp.zeros_like(notes)
    lead_high, lead_low = split_pair(lead)
    notes[0:1, : lead.shape[1]] = lead_high.astype(F32)
    notes[1:2, : lead.shape[1]] = lead_low.astype(F32)
    if has_own:
        groups = chunks // len(PARTS[0])
        per = chunks // groups
        start = pl.multiple_of(((groups - 1 - q) * per + per - 1) * 16, 16)
        block = far[pl.ds(start, 16), :width]
        x_own[...] = block
        own_high, own_low = split_pair(matmul(router_w[:16], block, NT))
        notes[8:16, 0:16] = own_high[:8].astype(F32)
        notes[8:16, 128:144] = own_low[:8].astype(F32)
    for step, out in enumerate((own, send1, send2, send3)):
        rows_of = pl.ds(pl.multiple_of((t ^ step) * share, share), share)
        both = jnp.concatenate([gate_w[rows_of, :], up_w[rows_of, :]], 0)
        out[:slots, : 2 * share] = matmul(x_slot[...], both, NT).astype(out.dtype)
        out[:slots, 2 * share :] = matmul(g_slot[...], down_w[rows_of, :], NT).astype(out.dtype)
        out[slots:] = notes[...].astype(out.dtype)


def act_kernel(slots, share, own, got1, got2, got3, toward, packed, weight, own_logits):
    total = own[...] + got1[...].astype(F32) + got2[...].astype(F32) + got3[...].astype(F32)
    notes = total[slots:]
    own_logits[...] = notes[8:16, :128] + notes[8:16, 128:256]
    used = jnp.sum(jnp.abs(toward[...]), axis=1, keepdims=True) > 0.5
    lead = to_column(notes[0:1] + notes[1:2], slots)
    w = jnp.where(used, jax.nn.sigmoid(lead), 0.0)
    weight[...] = w
    gate_proj, up_proj, back_proj = (
        total[:slots, k * share : (k + 1) * share] for k in range(3)
    )
    gate_sig = jax.nn.sigmoid(gate_proj)
    silu_gate = gate_proj * gate_sig
    scaled = w * back_proj
    packed[:slots, :share] = (
        scaled * up_proj * gate_sig * (1.0 + gate_proj * (1.0 - gate_sig))
    ).astype(BF)
    packed[:slots, share : 2 * share] = (scaled * silu_gate).astype(BF)
    packed[:slots, 2 * share :] = (w * silu_gate * up_proj).astype(BF)
    dgate_high, dgate_low = split_pair(to_row(silu_gate * up_proj * back_proj))
    lanes = dgate_high.shape[1]
    zero = jnp.zeros((14, lanes), F32)
    rows = jnp.concatenate([dgate_high.astype(F32), dgate_low.astype(F32), zero], 0)
    if lanes < 3 * share:
        rows = jnp.concatenate([rows, jnp.zeros((16, 3 * share - lanes), F32)], 1)
    packed[slots:] = rows.astype(BF)


def back_kernel(
    slots, share, has_own, place, p0, p1, p2, p3, gate_w, up_w, router_w, toward, weight, scatter,
    x_slot, extra, x_own, kept, sent, router_part,
):
    t = place[2]
    half = slots // 2
    tokens = scatter.shape[0] // 2
    pieces = (p0, p1, p2, p3)
    notes = sum(p[slots : slots + 16, :].astype(F32) for p in pieces)
    dgate = to_column(notes[0:1] + notes[1:2], slots)
    w = weight[...]
    coefficient = w * (1.0 - w) * dgate * toward[...]
    high, low = split_pair(coefficient)

    def gradient(part):
        pick = scatter[part * tokens : (part + 1) * tokens, :]
        rows = slice(part * half, (part + 1) * half)
        total = matmul(matmul(pick, high[rows]).astype(BF), router_w[...])
        total += matmul(matmul(pick, low[rows]).astype(BF), router_w[...])
        for step, piece in enumerate(pieces):
            rows_of = pl.ds(pl.multiple_of((t ^ step) * share, share), share)
            both = jnp.concatenate([gate_w[rows_of, :], up_w[rows_of, :]], 0)
            spread = matmul(pick, piece[rows, : 2 * share]).astype(BF)
            total += matmul(spread, both)
        return total

    sent[:tokens] = gradient(1).astype(BF)
    kept[...] = gradient(0)
    router = matmul(high, x_slot[...], TN)[:8] + matmul(low, x_slot[...], TN)[:8]
    if has_own:
        local_high, local_low = split_pair(extra[...])
        router += matmul(local_high, x_own[...], TN)[:8] + matmul(local_low, x_own[...], TN)[:8]
        router_part[...] = router
    else:
        router += extra[...]
        router_part[...] = router
        router_high, router_low = split_pair(router)
        sent[tokens : tokens + 8] = router_high
        sent[tokens + 8 :] = router_low


def pair_kernel(groups, has_router, kept, got, router_part, out):
    tokens = kept.shape[0]
    per = tokens // groups
    pair = (kept[...] + got[:tokens].astype(F32)).astype(BF)
    for j in range(groups):
        out[j, :per] = pair[j * per : (j + 1) * per]
    if has_router:
        router = router_part[...] + got[tokens : tokens + 8].astype(F32)
        router += got[tokens + 8 :].astype(F32)
        high, low = split_pair(router)
        both = jnp.concatenate([high, low], 0)
        for j in range(groups):
            out[j, per:] = both


def weight_kernel(parts, slots, share, place, *refs):
    t = place[2]
    inputs, (gate_grad, up_grad, down_grad) = refs[:-3], refs[-3:]
    for step in range(4):
        rows_of = pl.ds(pl.multiple_of((t ^ step) * share, share), share)
        both = down = 0.0
        for part in range(parts):
            block = inputs[part * 6 : part * 6 + 6]
            piece, x_slot, g_slot = block[step], block[4], block[5]
            both += matmul(piece[:slots, : 2 * share], x_slot[...], TN)
            down += matmul(piece[:slots, 2 * share :], g_slot[...], TN)
        gate_grad[rows_of, :] = both[:share].astype(BF)
        up_grad[rows_of, :] = both[share:].astype(BF)
        down_grad[rows_of, :] = down.astype(BF)


def call(body, ins, outs, flops, scratch=()):
    bytes_moved = sum(v.size * v.dtype.itemsize for v in ins)
    return pl.pallas_call(
        body,
        in_specs=[SMEM if v.ndim == 1 else VMEM for v in ins],
        out_specs=[VMEM] * len(outs),
        out_shape=[jax.ShapeDtypeStruct(shape, dtype) for shape, dtype in outs],
        scratch_shapes=list(scratch),
        cost_estimate=pl.CostEstimate(
            flops=flops, bytes_accessed=bytes_moved, transcendentals=0
        ),
        compiler_params=pltpu.CompilerParams(vmem_limit_bytes=40 * 2**20),
    )(*ins)


def exchange(value, axis, step):
    count = lax.axis_size(axis)
    return lax.ppermute(value, axis, [(k, k ^ step) for k in range(count)])


def spread_out(value, axis):
    count = lax.axis_size(axis)
    return lax.all_to_all(jnp.broadcast_to(value[None], (count, *value.shape)), axis, 0, 0)


def shards(stash, out_grad, router_weight, gate_weight, up_weight, down_weight, expert_ids):
    e, q = lax.axis_index("e"), lax.axis_index("q")
    experts, groups, ways = lax.axis_size("e"), lax.axis_size("q"), lax.axis_size("t")
    tokens, width = stash.shape[1], stash.shape[2]
    hidden = gate_weight.shape[0]
    share = hidden // ways
    ids = expert_ids[0]
    x_here, g_own = stash[0], out_grad[0]
    place = jnp.stack([e, q, lax.axis_index("t")]).astype(jnp.int32)
    router_tall = jnp.pad(router_weight, ((0, 128 - experts), (0, 0)))
    per = len(PARTS[0])
    chunks = groups * per
    slots = 2 * chunks * CAP

    id_columns = jnp.pad(ids.astype(BF), ((tokens, 0), (0, 126)))
    own = jnp.concatenate([jnp.concatenate([x_here, g_own], 0), id_columns], 1)
    quad = [own] + [exchange(own, "e", step) for step in range(1, experts)]
    work = []
    for index, part in enumerate(PARTS):
        near = spread_out(jnp.concatenate([quad[k] for k in part], 0), "q")
        near = near.reshape(chunks * 16, width + 128)
        work.append((near, exchange(near, "c", 1)))

    sums = []
    for index, (near, far) in enumerate(work):
        height = slots + 16
        outs = (
            [((height, 3 * share), F32)]
            + [((height, 3 * share), BF)] * 3
            + [((slots, width), BF)] * 2
            + [((slots, 128), F32), ((chunks * 16, slots // 2), BF), ((16, width), BF)]
        )
        mine, *sends, x_slot, g_slot, toward, scatter, x_own = call(
            functools.partial(project_kernel, chunks, width, share, index == 0),
            [place, near, far, gate_weight, up_weight, down_weight, router_tall],
            outs,
            2 * slots * width * (3 * hidden + 4 * chunks * 16),
            [pltpu.VMEM((16, 3 * share), F32)],
        )
        got = [exchange(value, "t", step + 1) for step, value in enumerate(sends)]
        sums.append((mine, got, x_slot, g_slot, toward, scatter, x_own))

    packs = []
    for index, (mine, got, x_slot, g_slot, toward, scatter, x_own) in enumerate(sums):
        packed, weight, own_logits = call(
            functools.partial(act_kernel, slots, share),
            [mine, *got, toward],
            [((slots + 16, 3 * share), BF), ((slots, 128), F32), ((8, 128), F32)],
            slots * share * 40,
        )
        pieces = [packed] + [exchange(packed, "t", step) for step in range(1, ways)]
        packs.append((pieces, weight, own_logits))

    own_logits = packs[0][2][:experts, :tokens].T
    expert_labels = jnp.arange(experts, dtype=jnp.int32)
    exp_logits = jnp.exp(own_logits)
    exp_total = jnp.sum(exp_logits, axis=1, keepdims=True)
    log_total = jnp.log(exp_total)
    prob_rows = exp_logits / exp_total
    counts = jnp.sum((ids.reshape(-1, 1) == expert_labels).astype(F32), axis=0)
    fraction = counts / (2.0 * tokens)
    balance_pull = BALANCE_WEIGHT * experts * fraction[None, :]
    local_part = 2.0 * Z_WEIGHT * log_total * prob_rows + prob_rows * (
        balance_pull - jnp.sum(prob_rows * balance_pull, axis=1, keepdims=True)
    )
    losses = jnp.stack(
        [
            jnp.mean(log_total[:, 0] * log_total[:, 0]),
            experts * jnp.sum(fraction * jnp.mean(prob_rows, axis=0)),
        ]
    )
    extra = jnp.pad(local_part, ((0, 16 - tokens), (0, 128 - experts)))

    x_own = sums[0][6]
    rows_back = []
    last = len(PARTS) - 1
    for index, (pieces, weight, _) in enumerate(packs):
        _, _, x_slot, _, toward, scatter, _ = sums[index]
        has_own, has_router = index == 0, index == last
        kept, sent, extra = call(
            functools.partial(back_kernel, slots, share, has_own),
            [place, *pieces, gate_weight, up_weight, router_tall, toward, weight, scatter, x_slot, extra, x_own],
            [
                ((chunks * 8, width), F32),
                ((chunks * 8 + 16 * (not has_own), width), BF),
                ((8, width), F32),
            ],
            2 * chunks * 16 * width * 2 * hidden,
        )
        got = exchange(sent, "c", 1)
        (pair,) = call(
            functools.partial(pair_kernel, groups, has_router),
            [kept, got, extra],
            [((groups, per * 8 + 16 * has_router, width), BF)],
            chunks * 8 * width * 2,
        )
        rows_back.append(lax.all_to_all(pair, "q", 0, 0).astype(F32).sum(0))

    router_part = rows_back[last][per * 8 : per * 8 + 8] + rows_back[last][per * 8 + 8 :]
    router_high = lax.reduce_precision(router_part, 8, 7)
    router_rows = jnp.concatenate([router_high, router_part - router_high], 0)
    dx_rows = {
        k: rows_back[index][j * 8 : j * 8 + 8]
        for index, part in enumerate(PARTS)
        for j, k in enumerate(part)
    }
    expert_dx = dx_rows[0]
    router_grad = router_part
    for step in range(1, experts):
        sent = jnp.concatenate([dx_rows[step], router_rows], 0).astype(BF)
        got = exchange(sent, "e", step).astype(F32)
        expert_dx = expert_dx + got[:8]
        router_grad = router_grad + (got[8:16] + got[16:])
    rw = router_weight.astype(F32)
    router_dx = jnp.dot(local_part, rw, precision=HIGH)
    in_grad = (g_own.astype(F32) + expert_dx + router_dx).astype(BF)

    inputs = [place]
    for (pieces, _, _), part in zip(packs, sums):
        inputs += [*pieces, part[2], part[3]]
    gate_grad, up_grad, down_grad = call(
        functools.partial(weight_kernel, len(PARTS), slots, share),
        inputs,
        [((hidden, width), BF)] * 3,
        2 * len(PARTS) * slots * width * hidden * 3,
    )
    return in_grad[None], gate_grad, up_grad, down_grad, router_grad[:experts], losses[None]


def solution(mesh):
    sections, ways = mesh.devices.shape
    experts, cores = 4, 2
    groups = sections // (experts * cores)
    fine = Mesh(mesh.devices.reshape(experts, groups, cores, ways), ("e", "q", "c", "t"))
    section = ("e", "q", "c")
    in_specs = (
        P(section, None, "t"),
        P(section, None, "t"),
        P(None, "t"),
        P(section, "t"),
        P(section, "t"),
        P(section, "t"),
        P(section, None, None),
    )
    out_specs = (
        P(section, None, "t"),
        P(section, "t"),
        P(section, "t"),
        P(section, "t"),
        P(None, "t"),
        P(section, None),
    )
    return jax.shard_map(shards, mesh=fine, in_specs=in_specs, out_specs=out_specs, check_vma=False)
```

```python
import functools

import jax
import jax.numpy as jnp
import numpy as np
from jax import lax
from jax.experimental import pallas as pl
from jax.experimental.pallas import tpu as pltpu
from jax.sharding import Mesh, PartitionSpec as P

CAP = 5
Z_WEIGHT = 0.25
BALANCE_WEIGHT = 1.0
BF = jnp.bfloat16
F32 = jnp.float32
GROUPS = 8
VMEM_LIMIT = 16 * 2**20
VMEM = pl.BlockSpec(memory_space=pltpu.VMEM)
NT = (((1,), (1,)), ((), ()))
TN = (((0,), (0,)), ((), ()))


def matmul(a, b, dims=(((1,), (0,)), ((), ()))):
    return lax.dot_general(a, b, dims, preferred_element_type=F32)


def split_pair(value):
    high = value.astype(BF)
    return high, (value - high.astype(F32)).astype(BF)


def up_to(count, step):
    return -(-count // step) * step


def to_row(value):
    count = value.shape[0]
    padded = up_to(count, 128)
    if padded > count:
        value = jnp.concatenate([value, jnp.zeros((padded - count, 128), F32)], 0)
    return jnp.sum(value.T, axis=0, keepdims=True)


def to_column(row, count):
    padded = up_to(count, 128)
    return jnp.broadcast_to(row[:, :padded], (128, padded)).T[:count]


def row_pair(value, lanes):
    high, low = split_pair(to_row(value))
    rows = jnp.concatenate([high.astype(F32), low.astype(F32), jnp.zeros((6, high.shape[1]), F32)], 0)
    if rows.shape[1] < lanes:
        rows = jnp.concatenate([rows, jnp.zeros((8, lanes - rows.shape[1]), F32)], 1)
    return rows


def spots(ids, expert, row):
    first = jnp.broadcast_to(ids[:, 0:1], ids.shape)
    second = jnp.broadcast_to(ids[:, 1:2], ids.shape)
    match = (first == expert) | (second == expert)
    matched = match.astype(F32)
    position = matched
    for step in (1, 2, 4):
        moved = pltpu.roll(position, step, 0)
        position = position + jnp.where((row & 7) >= step, moved, 0.0)
    return match, position - matched, first + second - expert


def pick_kernel(width, b0, b1, b2, b3, out):
    e_value = lax.axis_index("e").astype(F32)
    blocks = jnp.concatenate([b0[...], b1[...], b2[...], b3[...]], 0)
    rows = blocks.shape[0]
    row = lax.broadcasted_iota(jnp.int32, (rows, 128), 0)
    lane = lax.broadcasted_iota(jnp.int32, (rows, 128), 1).astype(F32)
    match, position, other = spots(blocks[:, width:].astype(F32), e_value, row)
    is_grad = (row & 8) > 0
    slot = (row >> 4).astype(F32) * CAP + position + jnp.where(is_grad, 4.0 * CAP, 0.0)
    slot = jnp.where(match, slot, -1.0)
    labels = lax.broadcasted_iota(jnp.int32, (rows, 8 * CAP), 1).astype(F32)
    pick = (jnp.broadcast_to(slot[:, 0:1], (rows, 8 * CAP)) == labels).astype(F32).astype(BF)
    sign = (lane == e_value).astype(F32) - (lane == other).astype(F32)
    sign = jnp.where(match & jnp.logical_not(is_grad), sign, 0.0).astype(BF)
    values = matmul(pick, blocks[:, :width], TN).astype(BF)
    signs = matmul(pick, sign, TN).astype(BF)
    for j in range(GROUPS):
        out[j, :, :width] = values
        out[j, :, width:] = signs


def project_kernel(
    width, share, has_own, block, gate_w, up_w, down_w, router_w, packer, own_block,
    own, send1, send2, send3, chosen, notes,
):
    t = lax.axis_index("t")
    slots = packer.shape[0] // 2
    taken = matmul(packer[:slots, :], block[...])
    x_slot, toward = taken[:, :width].astype(BF), taken[:, width:]
    g_slot = matmul(packer[slots:, :], block[:, :width]).astype(BF)
    chosen[:slots] = x_slot
    chosen[slots:] = g_slot
    lead = matmul(x_slot, router_w[...], NT) * toward
    notes[0:8] = row_pair(lead, 3 * share)
    notes[8:16] = jnp.zeros((8, 3 * share), F32)
    if has_own:
        own_high, own_low = split_pair(matmul(router_w[:16], own_block[:, :width], NT))
        notes[8:16, 0:16] = own_high[:8].astype(F32)
        notes[8:16, 128:144] = own_low[:8].astype(F32)
    own[:slots, 3 * share :] = toward
    own[slots:, 3 * share :] = jnp.zeros((16, 128), F32)
    for step, out in enumerate((own, send1, send2, send3)):
        rows_of = pl.ds(pl.multiple_of((t ^ step) * share, share), share)
        both = jnp.concatenate([gate_w[rows_of, :], up_w[rows_of, :]], 0)
        out[:slots, : 2 * share] = matmul(x_slot, both, NT).astype(out.dtype)
        out[:slots, 2 * share : 3 * share] = matmul(g_slot, down_w[rows_of, :], NT).astype(out.dtype)
        out[slots:, : 3 * share] = notes[...].astype(out.dtype)


def act_kernel(
    width, slots, share, experts, has_own, own_block, own, got1, got2, got3,
    packed, weight, local, losses,
):
    total = own[:, : 3 * share] + got1[...].astype(F32) + got2[...].astype(F32) + got3[...].astype(F32)
    toward = own[:slots, 3 * share :]
    used = jnp.sum(jnp.abs(toward), axis=1, keepdims=True) > 0.5
    lead = to_column(total[slots : slots + 1] + total[slots + 1 : slots + 2], slots)
    w = jnp.where(used, jax.nn.sigmoid(lead), 0.0)
    weight[...] = w * (1.0 - w) * toward
    gate_proj, up_proj, back_proj = (
        total[:slots, k * share : (k + 1) * share] for k in range(3)
    )
    gate_sig = jax.nn.sigmoid(gate_proj)
    silu_gate = gate_proj * gate_sig
    scaled = w * back_proj
    packed[:slots, :share] = (
        scaled * up_proj * gate_sig * (1.0 + gate_proj * (1.0 - gate_sig))
    ).astype(BF)
    packed[:slots, share : 2 * share] = (scaled * silu_gate).astype(BF)
    packed[:slots, 2 * share :] = (w * silu_gate * up_proj).astype(BF)
    rows = row_pair(silu_gate * up_proj * back_proj, 3 * share)
    packed[slots:] = jnp.concatenate([rows, jnp.zeros((8, 3 * share), F32)], 0).astype(BF)
    if not has_own:
        local[...] = jnp.zeros_like(local)
        losses[...] = jnp.zeros_like(losses)
        return

    logits = total[slots + 8 :, :128] + total[slots + 8 :, 128:256]
    expert = lax.broadcasted_iota(jnp.int32, (8, 128), 0)
    real = lax.broadcasted_iota(jnp.int32, (8, 128), 1) < 8
    exp_logits = jnp.where(expert < experts, jnp.exp(logits), 0.0)
    exp_total = jnp.sum(exp_logits, axis=0, keepdims=True)
    log_total = jnp.log(exp_total)
    prob = exp_logits / exp_total
    fraction = jnp.zeros((8, 128), F32)
    ids = own_block[:, width:].astype(F32)[:8]
    for k in range(experts):
        named = (ids[:, 0:1] == k).astype(F32) + (ids[:, 1:2] == k).astype(F32)
        count = jnp.sum(named, axis=0, keepdims=True)
        fraction = jnp.where(expert == k, count / 16.0, fraction)
    pull = BALANCE_WEIGHT * experts * fraction
    inner = jnp.sum(prob * pull, axis=0, keepdims=True)
    rows = 2.0 * Z_WEIGHT * log_total * prob + prob * (pull - inner)
    local[:8] = jnp.where(real, rows, 0.0)
    local[8:] = jnp.zeros((8, 128), F32)
    z_term = jnp.where(real[:1], log_total * log_total, 0.0)
    z_loss = jnp.sum(z_term, axis=1, keepdims=True) / 8.0
    mean_prob = jnp.sum(jnp.where(real, prob, 0.0), axis=1, keepdims=True) / 8.0
    balance = experts * jnp.sum(fraction[:, :1] * mean_prob, axis=0, keepdims=True)
    losses[0:1, 0:1] = z_loss
    losses[0:1, 1:2] = balance


def pair_rows(router):
    high, low = split_pair(router)
    return jnp.concatenate([high.astype(F32), low.astype(F32)], 0).astype(BF)


def slot_gradient(share, pieces, gate_w, up_w, router_w, weight):
    t = lax.axis_index("t")
    slots = weight.shape[0]
    notes = sum(p[slots : slots + 16, :].astype(F32) for p in pieces)
    high, low = split_pair(to_column(notes[0:1] + notes[1:2], slots) * weight[...])
    total = matmul(high, router_w[...]) + matmul(low, router_w[...])
    for step, piece in enumerate(pieces):
        rows_of = pl.ds(pl.multiple_of((t ^ step) * share, share), share)
        both = jnp.concatenate([gate_w[rows_of, :], up_w[rows_of, :]], 0)
        total += matmul(piece[:slots, : 2 * share], both)
    return total, high, low


def near_kernel(
    width, share, p0, p1, p2, p3, gate_w, up_w, router_w, weight, chosen, local, own_block,
    kept, router_part,
):
    total, high, low = slot_gradient(
        share, (p0, p1, p2, p3), gate_w, up_w, router_w, weight
    )
    slots = total.shape[0]
    kept[...] = total
    x_slot = chosen[:slots]
    router = matmul(high, x_slot, TN)[:8] + matmul(low, x_slot, TN)[:8]
    local_high, local_low = split_pair(local[...])
    router += matmul(local_high[:, :16], own_block[:, :width])[:8]
    router += matmul(local_low[:, :16], own_block[:, :width])[:8]
    router_part[...] = router


def far_kernel(
    share, p0, p1, p2, p3, gate_w, up_w, router_w, weight, chosen, router_near,
    sent, router_part,
):
    total, high, low = slot_gradient(
        share, (p0, p1, p2, p3), gate_w, up_w, router_w, weight
    )
    slots = total.shape[0]
    sent[:slots] = total.astype(BF)
    x_slot = chosen[:slots]
    router = router_near[...]
    router += matmul(high, x_slot, TN)[:8] + matmul(low, x_slot, TN)[:8]
    router_part[...] = router
    sent[slots:] = pair_rows(router)


def pair_kernel(kept, got, router_part, unpacker, out):
    half = kept.shape[0]
    pair = (kept[...] + got[:half].astype(F32)).astype(BF)
    rows = got[half:].astype(F32)
    router = (router_part[...] + rows[:8] + rows[8:]).astype(BF).astype(F32)
    router = jnp.concatenate([router, jnp.zeros_like(router)], 0).astype(BF)
    out[...] = matmul(unpacker[...], jnp.concatenate([pair, router], 0)).astype(BF)


def group_kernel(got, own, router_part, send1, send2, send3):
    total = got[0].astype(F32)
    for j in range(1, GROUPS):
        total += got[j].astype(F32)
    count = total.shape[0]
    row = lax.broadcasted_iota(jnp.int32, (8, total.shape[1]), 0)
    router = jnp.where(row < 4, pltpu.roll(total, 4, 0)[:8], 0.0)
    router_part[...] = router
    own[...] = total[:8]
    high = router.astype(BF).astype(F32)
    both = high + pltpu.roll(router - high, 4, 0)
    for step, out in enumerate((send1, send2, send3)):
        shifted = pltpu.roll(total, count - CAP * (step + 1), 0)
        out[...] = jnp.concatenate([shifted[:8], both], 0).astype(BF)


def final_kernel(
    width, experts, own, router_part, got1, got2, got3, own_block, local, router_w,
    in_grad, router_grad,
):
    e = lax.axis_index("e")
    ids = own_block[:, width:].astype(F32)[:8]
    row = lax.broadcasted_iota(jnp.int32, (8, 128), 0)
    total = own_block[8:, :width].astype(F32)
    router = router_part[...]
    for step in range(4):
        if step == 0:
            rows = own[...]
        else:
            both = (got1, got2, got3)[step - 1][...].astype(F32)
            rows = both[:8]
            router += both[8:] + pltpu.roll(both[8:], 4, 0)
        match, position, _ = spots(ids, (e ^ step).astype(F32), row)
        for k in range(CAP):
            chosen = (match & (position == k)).astype(F32)[:, 0:1]
            total += chosen * rows[k : k + 1]
    high, low = split_pair(local[...])
    rw = router_w[:16]
    total += matmul(high, rw, TN)[:8] + matmul(low, rw, TN)[:8]
    in_grad[...] = total.astype(BF)
    router_grad[...] = router[:experts]


def weight_kernel(slots, share, *refs):
    t = lax.axis_index("t")
    near, far, (gate_grad, up_grad, down_grad) = refs[:5], refs[5:10], refs[10:]
    for step in range(4):
        rows_of = pl.ds(pl.multiple_of((t ^ step) * share, share), share)
        both = down = 0.0
        for part in (near, far):
            piece, chosen = part[step], part[4]
            both += matmul(piece[:slots, : 2 * share], chosen[:slots], TN)
            down += matmul(piece[:slots, 2 * share :], chosen[slots:], TN)
        gate_grad[rows_of, :] = both[:share].astype(BF)
        up_grad[rows_of, :] = both[share:].astype(BF)
        down_grad[rows_of, :] = down.astype(BF)


def call(body, ins, outs, flops, scratch=()):
    bytes_moved = sum(v.size * v.dtype.itemsize for v in ins)
    return pl.pallas_call(
        body,
        in_specs=[VMEM] * len(ins),
        out_specs=[VMEM] * len(outs),
        out_shape=[jax.ShapeDtypeStruct(shape, dtype) for shape, dtype in outs],
        scratch_shapes=list(scratch),
        cost_estimate=pl.CostEstimate(
            flops=flops, bytes_accessed=bytes_moved, transcendentals=0
        ),
        compiler_params=pltpu.CompilerParams(vmem_limit_bytes=VMEM_LIMIT),
    )(*ins)


def exchange(value, axis, step):
    count = lax.axis_size(axis)
    return lax.ppermute(value, axis, [(k, k ^ step) for k in range(count)])


def packers(experts):
    per = experts * CAP
    pack = np.zeros((2, GROUPS, per, GROUPS, 2 * per), np.float32)
    unpack = np.zeros((GROUPS, per + 4, GROUPS * per + 16), np.float32)
    for j in range(GROUPS):
        for k in range(per):
            pack[0, j, k, j, k] = 1.0
            pack[1, j, k, j, per + k] = 1.0
            unpack[j, k, j * per + k] = 1.0
        for k in range(4):
            unpack[j, per + k, GROUPS * per + k] = 1.0
    pack = pack.reshape(2 * GROUPS * per, GROUPS * 2 * per)
    unpack = unpack.reshape(GROUPS * (per + 4), GROUPS * per + 16)
    return jnp.asarray(pack, BF), jnp.asarray(unpack, BF)


def shards(stash, out_grad, router_weight, gate_weight, up_weight, down_weight, expert_ids):
    experts, ways = lax.axis_size("e"), lax.axis_size("t")
    tokens, width = stash.shape[1], stash.shape[2]
    hidden = gate_weight.shape[0]
    share = hidden // ways
    router_tall = jnp.pad(router_weight, ((0, 128 - experts), (0, 0)))
    packer, unpacker = packers(experts)
    slots = GROUPS * experts * CAP
    height = slots + 16

    sections = experts * GROUPS * 2
    x_own = lax.ppermute(stash[0], ("e", "q", "c"), [(k, sections - 1 - k) for k in range(sections)])
    id_columns = jnp.pad(jnp.concatenate([expert_ids[0]] * 2, 0).astype(BF), ((0, 0), (0, 126)))
    own_block = jnp.concatenate([jnp.concatenate([x_own, out_grad[0]], 0), id_columns], 1)
    quad = [own_block] + [exchange(own_block, "e", step) for step in range(1, experts)]
    (chosen,) = call(
        functools.partial(pick_kernel, width),
        quad,
        [((GROUPS, 2 * experts * CAP, width + 128), BF)],
        4 * width * 64 * 40,
    )
    near = lax.all_to_all(chosen, "q", 0, 0).reshape(2 * slots, width + 128)
    far = exchange(near, "c", 1)

    halves = []
    for index, block in enumerate((near, far)):
        if index == 1:
            block, _ = lax.optimization_barrier((block, halves[0][2]))
        mine, *sends, taken = call(
            functools.partial(project_kernel, width, share, index == 0),
            [block, gate_weight, up_weight, down_weight, router_tall, packer, own_block],
            [((height, 3 * share + 128), F32)]
            + [((height, 3 * share), BF)] * 3
            + [((2 * slots, width), BF)],
            2 * slots * width * (3 * hidden + 4 * slots),
            [pltpu.VMEM((16, 3 * share), F32)],
        )
        got = [exchange(value, "t", step + 1) for step, value in enumerate(sends)]
        halves.append((mine, got, taken))
    gradients = []
    for index, (mine, got, taken) in enumerate(halves):
        packed, weight, local, losses = call(
            functools.partial(act_kernel, width, slots, share, experts, index == 0),
            [own_block, mine, *got],
            [((height, 3 * share), BF), ((slots, 128), F32), ((16, 128), F32), ((1, 2), F32)],
            slots * share * 40,
        )
        pieces = [packed] + [exchange(packed, "t", step) for step in range(1, ways)]
        gradients.append((pieces, weight, local, losses))
    _, _, local, losses = gradients[0]

    pieces, weight, _, _ = gradients[0]
    kept, router_near = call(
        functools.partial(near_kernel, width, share),
        [*pieces, gate_weight, up_weight, router_tall, weight, halves[0][2], local, own_block],
        [((slots, width), F32), ((8, width), F32)],
        2 * slots * width * 2 * hidden,
    )
    pieces, weight, _, _ = gradients[1]
    sent, router_part = call(
        functools.partial(far_kernel, share),
        [*pieces, gate_weight, up_weight, router_tall, weight, halves[1][2], router_near],
        [((height, width), BF), ((8, width), F32)],
        2 * slots * width * 2 * hidden,
    )
    got = exchange(sent, "c", 1)
    (pair,) = call(
        pair_kernel,
        [kept, got, router_part, unpacker],
        [((unpacker.shape[0], width), BF)],
        2 * slots * slots * width,
    )
    got = lax.all_to_all(pair.reshape(GROUPS, -1, width), "q", 0, 0)
    own_rows, router_part, *sends = call(
        group_kernel,
        [got],
        [((8, width), F32), ((8, width), F32)] + [((16, width), BF)] * 3,
        slots * width * 2,
    )
    gate_grad, up_grad, down_grad = call(
        functools.partial(weight_kernel, slots, share),
        [*gradients[0][0], halves[0][2], *gradients[1][0], halves[1][2]],
        [((hidden, width), BF)] * 3,
        4 * slots * width * hidden * 3,
    )
    got = [exchange(value, "e", step + 1) for step, value in enumerate(sends)]
    in_grad, router_grad = call(
        functools.partial(final_kernel, width, experts),
        [own_rows, router_part, *got, own_block, local, router_tall],
        [((tokens, width), BF), ((experts, width), F32)],
        tokens * width * 50,
    )
    return in_grad[None], gate_grad, up_grad, down_grad, router_grad, losses


def solution(mesh):
    ways = mesh.devices.shape[1]
    experts, cores = 4, 2
    fine = Mesh(mesh.devices.reshape(experts, GROUPS, cores, ways), ("e", "q", "c", "t"))
    section = ("e", "q", "c")
    in_specs = (
        P(section, None, "t"),
        P(section, None, "t"),
        P(None, "t"),
        P(section, "t"),
        P(section, "t"),
        P(section, "t"),
        P(section, None, None),
    )
    out_specs = (
        P(section, None, "t"),
        P(section, "t"),
        P(section, "t"),
        P(section, "t"),
        P(None, "t"),
        P(section, None),
    )
    return jax.shard_map(shards, mesh=fine, in_specs=in_specs, out_specs=out_specs, check_vma=False)
```

```python
import functools

import jax
import jax.numpy as jnp
import numpy as np
from jax import lax
from jax.experimental import pallas as pl
from jax.experimental.pallas import tpu as pltpu
from jax.sharding import Mesh, PartitionSpec as P

CAP = 5
Z_WEIGHT = 0.25
BALANCE_WEIGHT = 1.0
BF = jnp.bfloat16
F32 = jnp.float32
CHIPS = 16
SENT_ROWS = 24
BACK_ROWS = 16
VMEM_LIMIT = 16 * 2**20
VMEM = pl.BlockSpec(memory_space=pltpu.VMEM)
NT = (((1,), (1,)), ((), ()))
TN = (((0,), (0,)), ((), ()))


def matmul(a, b, dims=(((1,), (0,)), ((), ()))):
    return lax.dot_general(a, b, dims, preferred_element_type=F32)


def split_pair(value):
    high = value.astype(BF)
    return high, (value - high.astype(F32)).astype(BF)


def up_to(count, step):
    return -(-count // step) * step


def to_row(value):
    count = value.shape[0]
    padded = up_to(count, 128)
    if padded > count:
        value = jnp.concatenate([value, jnp.zeros((padded - count, 128), F32)], 0)
    return jnp.sum(value.T, axis=0, keepdims=True)


def to_column(row, count):
    padded = up_to(count, 128)
    return jnp.broadcast_to(row[:, :padded], (128, padded)).T[:count]


def row_pair(value, lanes):
    high, low = split_pair(to_row(value))
    rows = jnp.concatenate([high.astype(F32), low.astype(F32), jnp.zeros((6, high.shape[1]), F32)], 0)
    if rows.shape[1] < lanes:
        rows = jnp.concatenate([rows, jnp.zeros((8, lanes - rows.shape[1]), F32)], 1)
    return rows


def spots(ids, expert, row):
    first = jnp.broadcast_to(ids[:, 0:1], ids.shape)
    second = jnp.broadcast_to(ids[:, 1:2], ids.shape)
    match = (first == expert) | (second == expert)
    matched = match.astype(F32)
    position = matched
    for step in (1, 2, 4):
        moved = pltpu.roll(position, step, 0)
        position = position + jnp.where((row & 7) >= step, moved, 0.0)
    return match, position - matched, first + second - expert


def ready_kernel(x, gate_w, up_w, down_w, out):
    out[...] = x[:, :128].astype(F32)


def pick_kernel(width, x0, x1, g0, g1, ready, out, own_block):
    first = lax.axis_index("h") * 2
    parts = []
    for x, g in ((x0, g0), (x1, g1)):
        parts += [jnp.concatenate([x[...], g[:, width:]], 1), g[...]]
    blocks = jnp.concatenate(parts, 0)
    own_block[...] = blocks[:16]
    rows, count = blocks.shape[0], out.shape[1]
    row = lax.broadcasted_iota(jnp.int32, (rows, 128), 0)
    lane = lax.broadcasted_iota(jnp.int32, (rows, 128), 1).astype(F32)
    is_grad = (row & 8) > 0
    labels = lax.broadcasted_iota(jnp.int32, (rows, count), 1).astype(F32)
    ids = blocks[:, width:].astype(F32)
    for side in range(2):
        e_value = (first + side).astype(F32)
        match, position, other = spots(ids, e_value, row)
        slot = (row >> 4).astype(F32) * CAP + position + jnp.where(is_grad, 2.0 * CAP, 0.0)
        slot = jnp.where(match, slot, -1.0)
        pick = (jnp.broadcast_to(slot[:, 0:1], (rows, count)) == labels).astype(F32).astype(BF)
        sign = (lane == e_value).astype(F32) - (lane == other).astype(F32)
        sign = jnp.where(match & jnp.logical_not(is_grad), sign, 0.0).astype(BF)
        values = matmul(pick, blocks[:, :width], TN).astype(BF)
        signs = matmul(pick, sign, TN).astype(BF)
        for j in range(side * CHIPS // 2, (side + 1) * CHIPS // 2):
            out[j, :, :width] = values
            out[j, :, width:] = signs


def project_kernel(
    width, share, has_own, block, gate_w, up_w, down_w, router_w, packer, own_block,
    own, send1, send2, send3, chosen, notes,
):
    t = lax.axis_index("t")
    slots = packer.shape[0] // 2
    taken = matmul(packer[:slots, :], block[...])
    x_slot, toward = taken[:, :width].astype(BF), taken[:, width:]
    g_slot = matmul(packer[slots:, :], block[:, :width]).astype(BF)
    chosen[:slots] = x_slot
    chosen[slots:] = g_slot
    lead = matmul(x_slot, router_w[...], NT) * toward
    notes[...] = row_pair(lead, 3 * share)
    if has_own:
        logits = matmul(router_w[:16], own_block[:, :width], NT)[:8]
        high = logits.astype(BF).astype(F32)
        notes[:, 2 * share : 2 * share + 16] = high + pltpu.roll(logits - high, 4, 0)
    own[:slots, 3 * share :] = toward
    own[slots:, 3 * share :] = jnp.zeros((8, 128), F32)
    for step, out in enumerate((own, send1, send2, send3)):
        rows_of = pl.ds(pl.multiple_of((t ^ step) * share, share), share)
        both = jnp.concatenate([gate_w[rows_of, :], up_w[rows_of, :]], 0)
        out[:slots, : 2 * share] = matmul(x_slot, both, NT).astype(out.dtype)
        out[:slots, 2 * share : 3 * share] = matmul(g_slot, down_w[rows_of, :], NT).astype(out.dtype)
        out[slots:, : 3 * share] = notes[...].astype(out.dtype)


def act_kernel(
    width, slots, share, experts, has_own, own_block, own, got1, got2, got3,
    packed, weight, local, losses,
):
    total = own[:, : 3 * share] + got1[...].astype(F32) + got2[...].astype(F32) + got3[...].astype(F32)
    toward = own[:slots, 3 * share :]
    used = jnp.sum(jnp.abs(toward), axis=1, keepdims=True) > 0.5
    lead = to_column(total[slots : slots + 1] + total[slots + 1 : slots + 2], slots)
    w = jnp.where(used, jax.nn.sigmoid(lead), 0.0)
    weight[...] = w * (1.0 - w) * toward
    gate_proj, up_proj, back_proj = (
        total[:slots, k * share : (k + 1) * share] for k in range(3)
    )
    gate_sig = jax.nn.sigmoid(gate_proj)
    silu_gate = gate_proj * gate_sig
    scaled = w * back_proj
    packed[:slots, :share] = (
        scaled * up_proj * gate_sig * (1.0 + gate_proj * (1.0 - gate_sig))
    ).astype(BF)
    packed[:slots, share : 2 * share] = (scaled * silu_gate).astype(BF)
    packed[:slots, 2 * share :] = (w * silu_gate * up_proj).astype(BF)
    rows = row_pair(silu_gate * up_proj * back_proj, 3 * share)
    packed[slots:] = rows.astype(BF)
    if not has_own:
        local[...] = jnp.zeros_like(local)
        losses[...] = jnp.zeros_like(losses)
        return

    logits = total[slots:, 2 * share : 3 * share]
    logits = logits + pltpu.roll(logits, 4, 0)
    expert = lax.broadcasted_iota(jnp.int32, (8, 128), 0)
    real = lax.broadcasted_iota(jnp.int32, (8, 128), 1) < 8
    exp_logits = jnp.where(expert < experts, jnp.exp(logits), 0.0)
    exp_total = jnp.sum(exp_logits, axis=0, keepdims=True)
    log_total = jnp.log(exp_total)
    prob = exp_logits / exp_total
    fraction = jnp.zeros((8, 128), F32)
    ids = own_block[:, width:].astype(F32)[:8]
    for k in range(experts):
        named = (ids[:, 0:1] == k).astype(F32) + (ids[:, 1:2] == k).astype(F32)
        count = jnp.sum(named, axis=0, keepdims=True)
        fraction = jnp.where(expert == k, count / 16.0, fraction)
    pull = BALANCE_WEIGHT * experts * fraction
    inner = jnp.sum(prob * pull, axis=0, keepdims=True)
    rows = 2.0 * Z_WEIGHT * log_total * prob + prob * (pull - inner)
    local[:8] = jnp.where(real, rows, 0.0)
    local[8:] = jnp.zeros((8, 128), F32)
    z_term = jnp.where(real[:1], log_total * log_total, 0.0)
    z_loss = jnp.sum(z_term, axis=1, keepdims=True) / 8.0
    mean_prob = jnp.sum(jnp.where(real, prob, 0.0), axis=1, keepdims=True) / 8.0
    balance = experts * jnp.sum(fraction[:, :1] * mean_prob, axis=0, keepdims=True)
    losses[0:1, 0:1] = z_loss
    losses[0:1, 1:2] = balance


def pair_rows(router):
    high, low = split_pair(router)
    return jnp.concatenate([high.astype(F32), low.astype(F32)], 0).astype(BF)


def slot_gradient(share, pieces, gate_w, up_w, router_w, weight):
    t = lax.axis_index("t")
    slots = weight.shape[0]
    notes = sum(p[slots:, :].astype(F32) for p in pieces)
    high, low = split_pair(to_column(notes[0:1] + notes[1:2], slots) * weight[...])
    total = matmul(high, router_w[...]) + matmul(low, router_w[...])
    for step, piece in enumerate(pieces):
        rows_of = pl.ds(pl.multiple_of((t ^ step) * share, share), share)
        both = jnp.concatenate([gate_w[rows_of, :], up_w[rows_of, :]], 0)
        total += matmul(piece[:slots, : 2 * share], both)
    return total, high, low


def near_kernel(
    width, share, p0, p1, p2, p3, gate_w, up_w, router_w, weight, chosen, local, own_block,
    kept, router_part,
):
    total, high, low = slot_gradient(
        share, (p0, p1, p2, p3), gate_w, up_w, router_w, weight
    )
    slots = total.shape[0]
    kept[...] = total
    x_slot = chosen[:slots]
    router = matmul(high, x_slot, TN)[:8] + matmul(low, x_slot, TN)[:8]
    local_high, local_low = split_pair(local[...])
    router += matmul(local_high[:, :16], own_block[:, :width])[:8]
    router += matmul(local_low[:, :16], own_block[:, :width])[:8]
    router_part[...] = router


def far_kernel(
    share, p0, p1, p2, p3, gate_w, up_w, router_w, weight, chosen, router_near,
    sent, router_part,
):
    total, high, low = slot_gradient(
        share, (p0, p1, p2, p3), gate_w, up_w, router_w, weight
    )
    slots = total.shape[0]
    sent[:slots] = total.astype(BF)
    x_slot = chosen[:slots]
    router = router_near[...]
    router += matmul(high, x_slot, TN)[:8] + matmul(low, x_slot, TN)[:8]
    router_part[...] = router
    sent[slots:] = pair_rows(router)


def pair_kernel(kept, got, router_part, unpacker, out):
    half = kept.shape[0]
    pair = (kept[...] + got[:half].astype(F32)).astype(BF)
    rows = got[half:].astype(F32)
    router = (router_part[...] + rows[:8] + rows[8:]).astype(BF).astype(F32)
    router = jnp.concatenate([router, jnp.zeros_like(router)], 0).astype(BF)
    out[...] = matmul(unpacker[...], jnp.concatenate([pair, router], 0)).astype(BF)


def group_kernel(got, own, router_part, send):
    sides = []
    for side in range(2):
        first = side * CHIPS // 2
        total = got[first].astype(F32)
        for j in range(first + 1, first + CHIPS // 2):
            total += got[j].astype(F32)
        own[8 * side : 8 * side + 8] = total[:8]
        sides.append(total)
    count = total.shape[0]
    row = lax.broadcasted_iota(jnp.int32, (8, total.shape[1]), 0)
    router = pltpu.roll(sides[0] + sides[1], count - 2 * CAP, 0)[:8]
    router = jnp.where(row < 4, router, 0.0)
    router_part[...] = router
    high = router.astype(BF).astype(F32)
    both = high + pltpu.roll(router - high, 4, 0)
    moved = [pltpu.roll(total, count - CAP, 0)[:8] for total in sides]
    send[...] = jnp.concatenate([*moved, both, jnp.zeros_like(both)], 0).astype(BF)


def final_kernel(
    width, experts, own, router_part, got, own_block, local, router_w, in_grad, router_grad
):
    h = lax.axis_index("h")
    ids = own_block[:, width:].astype(F32)[:8]
    row = lax.broadcasted_iota(jnp.int32, (8, 128), 0)
    total = own_block[8:, :width].astype(F32)
    other = got[...].astype(F32)
    router = router_part[...] + other[16:24] + pltpu.roll(other[16:24], 4, 0)
    for step, blocks in enumerate((own[...], other)):
        for side in range(2):
            rows = blocks[8 * side : 8 * side + 8]
            match, position, _ = spots(ids, ((h ^ step) * 2 + side).astype(F32), row)
            for k in range(CAP):
                chosen = (match & (position == k)).astype(F32)[:, 0:1]
                total += chosen * rows[k : k + 1]
    high, low = split_pair(local[...])
    rw = router_w[:16]
    total += matmul(high, rw, TN)[:8] + matmul(low, rw, TN)[:8]
    in_grad[...] = total.astype(BF)
    router_grad[...] = router[:experts]


def weight_kernel(slots, share, *refs):
    t = lax.axis_index("t")
    near, far, (gate_grad, up_grad, down_grad) = refs[:5], refs[5:10], refs[10:]
    for step in range(4):
        rows_of = pl.ds(pl.multiple_of((t ^ step) * share, share), share)
        both = down = 0.0
        for part in (near, far):
            piece, chosen = part[step], part[4]
            both += matmul(piece[:slots, : 2 * share], chosen[:slots], TN)
            down += matmul(piece[:slots, 2 * share :], chosen[slots:], TN)
        gate_grad[rows_of, :] = both[:share].astype(BF)
        up_grad[rows_of, :] = both[share:].astype(BF)
        down_grad[rows_of, :] = down.astype(BF)


def call(body, ins, outs, flops, scratch=()):
    bytes_moved = sum(v.size * v.dtype.itemsize for v in ins)
    return pl.pallas_call(
        body,
        in_specs=[VMEM] * len(ins),
        out_specs=[VMEM] * len(outs),
        out_shape=[jax.ShapeDtypeStruct(shape, dtype) for shape, dtype in outs],
        scratch_shapes=list(scratch),
        cost_estimate=pl.CostEstimate(
            flops=flops, bytes_accessed=bytes_moved, transcendentals=0
        ),
        compiler_params=pltpu.CompilerParams(vmem_limit_bytes=VMEM_LIMIT),
    )(*ins)


def exchange(value, axis, step):
    count = lax.axis_size(axis)
    return lax.ppermute(value, axis, [(k, k ^ step) for k in range(count)])


def packers():
    per, taken, sent = 2 * CAP, SENT_ROWS, BACK_ROWS
    pack = np.zeros((2, CHIPS, per, CHIPS, taken), np.float32)
    unpack = np.zeros((CHIPS, sent, CHIPS * per + 16), np.float32)
    for j in range(CHIPS):
        for k in range(per):
            pack[0, j, k, j, k] = 1.0
            pack[1, j, k, j, per + k] = 1.0
            unpack[j, k, j * per + k] = 1.0
        for k in range(4):
            unpack[j, per + k, CHIPS * per + k] = 1.0
    pack = pack.reshape(2 * CHIPS * per, CHIPS * taken)
    unpack = unpack.reshape(CHIPS * sent, CHIPS * per + 16)
    return jnp.asarray(pack, BF), jnp.asarray(unpack, BF)


def shards(stash, out_grad, router_weight, gate_weight, up_weight, down_weight, expert_ids):
    experts, ways = router_weight.shape[0], lax.axis_size("t")
    tokens, width = stash.shape[1], stash.shape[2]
    hidden = gate_weight.shape[0]
    share = hidden // ways
    router_tall = jnp.pad(router_weight, ((0, 128 - experts), (0, 0)))
    packer, unpacker = packers()
    slots = 2 * CHIPS * CAP
    height = slots + 8

    sections = 4 * CHIPS
    id_columns = jnp.pad(expert_ids[0].astype(BF), ((0, 0), (0, 126)))
    g_own = jnp.concatenate([out_grad[0], id_columns], 1)
    g_other = exchange(g_own, "h", 1)
    x_other, x_own = (
        lax.ppermute(
            stash[0],
            ("h", "p", "c"),
            [(k, (sections - 1 - k) ^ (step * sections // 2)) for k in range(sections)],
        )
        for step in (1, 0)
    )
    (ready,) = call(
        ready_kernel, [x_other, gate_weight, up_weight, down_weight], [((tokens, 128), F32)], 1000
    )
    chosen, own_block = call(
        functools.partial(pick_kernel, width),
        [x_own, x_other, g_own, g_other, ready],
        [((CHIPS, SENT_ROWS, width + 128), BF), ((2 * tokens, width + 128), BF)],
        8 * width * 32 * SENT_ROWS,
    )
    near = lax.all_to_all(chosen, "p", 0, 0).reshape(CHIPS * SENT_ROWS, width + 128)
    far = exchange(near, "c", 1)

    halves = []
    for index, block in enumerate((near, far)):
        if index == 1:
            block, _ = lax.optimization_barrier((block, halves[0][2]))
        mine, *sends, taken = call(
            functools.partial(project_kernel, width, share, index == 0),
            [block, gate_weight, up_weight, down_weight, router_tall, packer, own_block],
            [((height, 3 * share + 128), F32)]
            + [((height, 3 * share), BF)] * 3
            + [((2 * slots, width), BF)],
            2 * slots * width * (3 * hidden + 4 * slots),
            [pltpu.VMEM((8, 3 * share), F32)],
        )
        got = [exchange(value, "t", step + 1) for step, value in enumerate(sends)]
        halves.append((mine, got, taken))
    gradients = []
    for index, (mine, got, taken) in enumerate(halves):
        packed, weight, local, losses = call(
            functools.partial(act_kernel, width, slots, share, experts, index == 0),
            [own_block, mine, *got],
            [((height, 3 * share), BF), ((slots, 128), F32), ((16, 128), F32), ((1, 2), F32)],
            slots * share * 40,
        )
        pieces = [packed, exchange(packed, "t", 1), exchange(packed, "t", 2)]
        pieces.append(exchange(pieces[2], "t", 1))
        gradients.append((pieces, weight, local, losses))
    _, _, local, losses = gradients[0]

    pieces, weight, _, _ = gradients[0]
    kept, router_near = call(
        functools.partial(near_kernel, width, share),
        [*pieces, gate_weight, up_weight, router_tall, weight, halves[0][2], local, own_block],
        [((slots, width), F32), ((8, width), F32)],
        2 * slots * width * 2 * hidden,
    )
    pieces, weight, _, _ = gradients[1]
    sent, router_part = call(
        functools.partial(far_kernel, share),
        [*pieces, gate_weight, up_weight, router_tall, weight, halves[1][2], router_near],
        [((slots + 16, width), BF), ((8, width), F32)],
        2 * slots * width * 2 * hidden,
    )
    got = exchange(sent, "c", 1)
    (pair,) = call(
        pair_kernel,
        [kept, got, router_part, unpacker],
        [((unpacker.shape[0], width), BF)],
        2 * slots * slots * width,
    )
    got = lax.all_to_all(pair.reshape(CHIPS, -1, width), "p", 0, 0)
    own_rows, router_part, sent = call(
        group_kernel,
        [got],
        [((16, width), F32), ((8, width), F32), ((32, width), BF)],
        slots * width * 2,
    )
    gate_grad, up_grad, down_grad = call(
        functools.partial(weight_kernel, slots, share),
        [*gradients[0][0], halves[0][2], *gradients[1][0], halves[1][2]],
        [((hidden, width), BF)] * 3,
        4 * slots * width * hidden * 3,
    )
    in_grad, router_grad = call(
        functools.partial(final_kernel, width, experts),
        [own_rows, router_part, exchange(sent, "h", 1), own_block, local, router_tall],
        [((tokens, width), BF), ((experts, width), F32)],
        tokens * width * 50,
    )
    return in_grad[None], gate_grad, up_grad, down_grad, router_grad, losses


def solution(mesh):
    ways = mesh.devices.shape[1]
    fine = Mesh(mesh.devices.reshape(2, CHIPS, 2, ways), ("h", "p", "c", "t"))
    section = ("h", "p", "c")
    in_specs = (
        P(section, None, "t"),
        P(section, None, "t"),
        P(None, "t"),
        P(section, "t"),
        P(section, "t"),
        P(section, "t"),
        P(section, None, None),
    )
    out_specs = (
        P(section, None, "t"),
        P(section, "t"),
        P(section, "t"),
        P(section, "t"),
        P(None, "t"),
        P(section, None),
    )
    return jax.shard_map(shards, mesh=fine, in_specs=in_specs, out_specs=out_specs, check_vma=False)
```

```python
import functools

import jax
import jax.numpy as jnp
import numpy as np
from jax import lax
from jax.experimental import pallas as pl
from jax.experimental.pallas import tpu as pltpu
from jax.sharding import Mesh, PartitionSpec as P

CAP = 5
Z_WEIGHT = 0.25
BALANCE_WEIGHT = 1.0
BF = jnp.bfloat16
F32 = jnp.float32
CHIPS = 16
SENT_ROWS = 16
BACK_ROWS = 8
VMEM_LIMIT = 16 * 2**20
VMEM = pl.BlockSpec(memory_space=pltpu.VMEM)
NT = (((1,), (1,)), ((), ()))
TN = (((0,), (0,)), ((), ()))


def matmul(a, b, dims=(((1,), (0,)), ((), ()))):
    return lax.dot_general(a, b, dims, preferred_element_type=F32)


def split_pair(value):
    high = value.astype(BF)
    return high, (value - high.astype(F32)).astype(BF)


def up_to(count, step):
    return -(-count // step) * step


def to_row(value):
    count = value.shape[0]
    padded = up_to(count, 128)
    if padded > count:
        value = jnp.concatenate([value, jnp.zeros((padded - count, 128), F32)], 0)
    return jnp.sum(value.T, axis=0, keepdims=True)


def to_column(row, count):
    padded = up_to(count, 128)
    return jnp.broadcast_to(row[:, :padded], (128, padded)).T[:count]


def row_pair(value, lanes):
    high, low = split_pair(to_row(value))
    rows = jnp.concatenate([high.astype(F32), low.astype(F32), jnp.zeros((6, high.shape[1]), F32)], 0)
    if rows.shape[1] < lanes:
        rows = jnp.concatenate([rows, jnp.zeros((8, lanes - rows.shape[1]), F32)], 1)
    return rows


def spots(ids, expert, row):
    first = jnp.broadcast_to(ids[:, 0:1], ids.shape)
    second = jnp.broadcast_to(ids[:, 1:2], ids.shape)
    match = (first == expert) | (second == expert)
    matched = match.astype(F32)
    position = matched
    for step in (1, 2, 4):
        moved = pltpu.roll(position, step, 0)
        position = position + jnp.where((row & 7) >= step, moved, 0.0)
    return match, position - matched, first + second - expert


def ready_kernel(x, gate_w, up_w, down_w, out):
    out[...] = x[:, :128].astype(F32)


def pick_kernel(width, mine, got, ready, out, own_block):
    first = lax.axis_index("h") * 2
    parts = []
    for x, g in ((got, mine), (mine, got)):
        parts += [jnp.concatenate([x[:8, :width], g[8:, width:]], 1), g[8:, :]]
    blocks = jnp.concatenate(parts, 0)
    own_block[...] = blocks[:16]
    rows, quarter = blocks.shape[0], width // 4
    row = lax.broadcasted_iota(jnp.int32, (rows, 128), 0)
    lane = lax.broadcasted_iota(jnp.int32, (rows, 128), 1).astype(F32)
    grad = ((row & 8) >> 3).astype(F32)
    labels = lax.broadcasted_iota(jnp.int32, (rows, SENT_ROWS), 1).astype(F32)
    ids = blocks[:, width:].astype(F32)

    def pick(label):
        wide = jnp.broadcast_to(label[:, 0:1], (rows, SENT_ROWS))
        return (wide == labels).astype(F32).astype(BF)

    for side in range(2):
        e_value = (first + side).astype(F32)
        match, position, other = spots(ids, e_value, row)
        slot = (row >> 4).astype(F32) * CAP + position
        slot = jnp.where(match, slot, -100.0)
        main = jnp.where(slot < 8, slot + 8.0 * grad, -100.0)
        rest = jnp.where(slot >= 8, (slot - 8.0 + 2.0 * grad) * 4.0, -100.0)
        sign = (lane == e_value).astype(F32) - (lane == other).astype(F32)
        values = matmul(pick(main), blocks[:, :width], TN).astype(BF)
        extra = sum(
            matmul(pick(rest + m), blocks[:, m * quarter : (m + 1) * quarter], TN) for m in range(4)
        ).astype(BF)
        signs = matmul(pick(jnp.where(grad > 0, -100.0, slot)), sign.astype(BF), TN).astype(BF)
        for j in range(side * CHIPS // 2, (side + 1) * CHIPS // 2):
            out[j, :, :width] = values
            out[j, :, width : width + quarter] = extra
            out[j, :, width + quarter :] = signs


def project_kernel(
    width, share, has_own, block, gate_w, up_w, down_w, router_w, packer, own_block,
    own, send1, send2, send3, chosen, notes,
):
    t = lax.axis_index("t")
    slots, quarter = packer.shape[0] // 11, width // 4
    extra = block[:, width : width + quarter]

    def unpack(first):
        parts = []
        for m in range(4):
            taken = matmul(packer[first * slots : (first + 1) * slots, :], block[:, m * quarter : (m + 1) * quarter])
            rows = slice((first + 1 + m) * slots, (first + 2 + m) * slots)
            parts.append((taken + matmul(packer[rows, :], extra)).astype(BF))
        return jnp.concatenate(parts, 1)

    x_slot, g_slot = unpack(0), unpack(5)
    toward = matmul(packer[10 * slots :, :], block[:, width + quarter :])
    chosen[:slots] = x_slot
    chosen[slots:] = g_slot
    lead = matmul(x_slot, router_w[...], NT) * toward
    notes[...] = row_pair(lead, 3 * share)
    if has_own:
        logits = matmul(router_w[:16], own_block[:, :width], NT)[:8]
        high = logits.astype(BF).astype(F32)
        notes[:, 2 * share : 2 * share + 16] = high + pltpu.roll(logits - high, 4, 0)
    own[:slots, 3 * share :] = toward
    own[slots:, 3 * share :] = jnp.zeros((8, 128), F32)
    for step, out in enumerate((own, send1, send2, send3)):
        rows_of = pl.ds(pl.multiple_of((t ^ step) * share, share), share)
        both = jnp.concatenate([gate_w[rows_of, :], up_w[rows_of, :]], 0)
        out[:slots, : 2 * share] = matmul(x_slot, both, NT).astype(out.dtype)
        out[:slots, 2 * share : 3 * share] = matmul(g_slot, down_w[rows_of, :], NT).astype(out.dtype)
        out[slots:, : 3 * share] = notes[...].astype(out.dtype)


def act_kernel(
    width, slots, share, experts, has_own, own_block, own, got1, got2, got3,
    packed, weight, local, losses,
):
    total = own[:, : 3 * share] + got1[...].astype(F32) + got2[...].astype(F32) + got3[...].astype(F32)
    toward = own[:slots, 3 * share :]
    used = jnp.sum(jnp.abs(toward), axis=1, keepdims=True) > 0.5
    lead = to_column(total[slots : slots + 1] + total[slots + 1 : slots + 2], slots)
    w = jnp.where(used, jax.nn.sigmoid(lead), 0.0)
    weight[...] = w * (1.0 - w) * toward
    gate_proj, up_proj, back_proj = (
        total[:slots, k * share : (k + 1) * share] for k in range(3)
    )
    gate_sig = jax.nn.sigmoid(gate_proj)
    silu_gate = gate_proj * gate_sig
    scaled = w * back_proj
    packed[:slots, :share] = (
        scaled * up_proj * gate_sig * (1.0 + gate_proj * (1.0 - gate_sig))
    ).astype(BF)
    packed[:slots, share : 2 * share] = (scaled * silu_gate).astype(BF)
    packed[:slots, 2 * share :] = (w * silu_gate * up_proj).astype(BF)
    rows = row_pair(silu_gate * up_proj * back_proj, 3 * share)
    packed[slots:] = rows.astype(BF)
    if not has_own:
        local[...] = jnp.zeros_like(local)
        losses[...] = jnp.zeros_like(losses)
        return

    logits = total[slots:, 2 * share : 3 * share]
    logits = logits + pltpu.roll(logits, 4, 0)
    expert = lax.broadcasted_iota(jnp.int32, (8, 128), 0)
    real = lax.broadcasted_iota(jnp.int32, (8, 128), 1) < 8
    exp_logits = jnp.where(expert < experts, jnp.exp(logits), 0.0)
    exp_total = jnp.sum(exp_logits, axis=0, keepdims=True)
    log_total = jnp.log(exp_total)
    prob = exp_logits / exp_total
    fraction = jnp.zeros((8, 128), F32)
    ids = own_block[:, width:].astype(F32)[:8]
    for k in range(experts):
        named = (ids[:, 0:1] == k).astype(F32) + (ids[:, 1:2] == k).astype(F32)
        count = jnp.sum(named, axis=0, keepdims=True)
        fraction = jnp.where(expert == k, count / 16.0, fraction)
    pull = BALANCE_WEIGHT * experts * fraction
    inner = jnp.sum(prob * pull, axis=0, keepdims=True)
    rows = 2.0 * Z_WEIGHT * log_total * prob + prob * (pull - inner)
    local[:8] = jnp.where(real, rows, 0.0)
    local[8:] = jnp.zeros((8, 128), F32)
    z_term = jnp.where(real[:1], log_total * log_total, 0.0)
    z_loss = jnp.sum(z_term, axis=1, keepdims=True) / 8.0
    mean_prob = jnp.sum(jnp.where(real, prob, 0.0), axis=1, keepdims=True) / 8.0
    balance = experts * jnp.sum(fraction[:, :1] * mean_prob, axis=0, keepdims=True)
    losses[0:1, 0:1] = z_loss
    losses[0:1, 1:2] = balance


def pair_rows(router):
    high, low = split_pair(router)
    return jnp.concatenate([high.astype(F32), low.astype(F32)], 0).astype(BF)


def slot_gradient(share, pieces, gate_w, up_w, router_w, weight):
    t = lax.axis_index("t")
    slots = weight.shape[0]
    notes = sum(p[slots:, :].astype(F32) for p in pieces)
    high, low = split_pair(to_column(notes[0:1] + notes[1:2], slots) * weight[...])
    total = matmul(high, router_w[...]) + matmul(low, router_w[...])
    for step, piece in enumerate(pieces):
        rows_of = pl.ds(pl.multiple_of((t ^ step) * share, share), share)
        both = jnp.concatenate([gate_w[rows_of, :], up_w[rows_of, :]], 0)
        total += matmul(piece[:slots, : 2 * share], both)
    return total, high, low


def near_kernel(
    width, share, p0, p1, p2, p3, gate_w, up_w, router_w, weight, chosen, local, own_block,
    kept, router_part,
):
    total, high, low = slot_gradient(
        share, (p0, p1, p2, p3), gate_w, up_w, router_w, weight
    )
    slots = total.shape[0]
    kept[...] = total
    x_slot = chosen[:slots]
    router = matmul(high, x_slot, TN)[:8] + matmul(low, x_slot, TN)[:8]
    local_high, local_low = split_pair(local[...])
    router += matmul(local_high[:, :16], own_block[:, :width])[:8]
    router += matmul(local_low[:, :16], own_block[:, :width])[:8]
    router_part[...] = router


def far_kernel(
    share, p0, p1, p2, p3, gate_w, up_w, router_w, weight, chosen, router_near,
    sent, router_part,
):
    total, high, low = slot_gradient(
        share, (p0, p1, p2, p3), gate_w, up_w, router_w, weight
    )
    slots = total.shape[0]
    sent[:slots] = total.astype(BF)
    x_slot = chosen[:slots]
    router = router_near[...]
    router += matmul(high, x_slot, TN)[:8] + matmul(low, x_slot, TN)[:8]
    router_part[...] = router
    sent[slots:] = pair_rows(router)


def pair_kernel(width, kept, got, router_part, unpacker, out):
    half, quarter, count = kept.shape[0], width // 4, out.shape[0]
    pair = (kept[...] + got[:half].astype(F32)).astype(BF)
    rows = got[half:].astype(F32)
    router = (router_part[...] + rows[:8] + rows[8:]).astype(BF).astype(F32)
    router = jnp.concatenate([router, jnp.zeros_like(router)], 0).astype(BF)
    pair = jnp.concatenate([pair, router], 0)
    out[:, :width] = matmul(unpacker[:count, :], pair).astype(BF)
    for c in range(3):
        value = 0.0
        for m in range(4):
            first = (1 + 4 * c + m) * count
            value += matmul(
                unpacker[first : first + count, :], pair[:, m * quarter : (m + 1) * quarter]
            )
        out[:, width + c * quarter : width + (c + 1) * quarter] = value.astype(BF)


def group_kernel(width, got, own, router_part, send):
    quarter = width // 4
    row = lax.broadcasted_iota(jnp.int32, (8, quarter), 0)
    sides = []
    for side in range(2):
        first = side * CHIPS // 2
        total = got[first].astype(F32)
        for j in range(first + 1, first + CHIPS // 2):
            total += got[j].astype(F32)
        more = []
        for m in range(4):
            value = jnp.zeros((8, quarter), F32)
            for i in range(6):
                r, c = (4 * i + m) // 3, (4 * i + m) % 3
                piece = total[r : r + 1, width + c * quarter : width + (c + 1) * quarter]
                value = jnp.where(row == i, jnp.broadcast_to(piece, (8, quarter)), value)
            more.append(value)
        own[8 * side : 8 * side + 8] = total[:, :width]
        sides.append(jnp.concatenate([total[:, :width], jnp.concatenate(more, 1)], 0))
    near, far = sides
    row = lax.broadcasted_iota(jnp.int32, near.shape, 0)
    router_part[...] = pltpu.roll(near + far, 16 - 2 * CAP, 0)[:8]
    send[...] = jnp.where(
        row < CAP, pltpu.roll(near, 16 - CAP, 0), jnp.where(row < 2 * CAP, far, near + far)
    ).astype(BF)


def final_kernel(
    width, experts, own, router_part, got, own_block, local, router_w, in_grad, router_grad
):
    h = lax.axis_index("h")
    ids = own_block[:, width:].astype(F32)[:8]
    row = lax.broadcasted_iota(jnp.int32, (8, 128), 0)
    total = own_block[8:, :width].astype(F32)
    other = got[...].astype(F32)
    router = router_part[...] + pltpu.roll(other, 16 - 2 * CAP, 0)[:8]
    for step in range(2):
        for side in range(2):
            match, position, _ = spots(ids, ((h ^ step) * 2 + side).astype(F32), row)
            for k in range(CAP):
                chosen = (match & (position == k)).astype(F32)[:, 0:1]
                if step == 0:
                    value = own[8 * side + k : 8 * side + k + 1, :]
                else:
                    value = other[CAP * side + k : CAP * side + k + 1]
                total += chosen * value
    high, low = split_pair(local[...])
    rw = router_w[:16]
    total += matmul(high, rw, TN)[:8] + matmul(low, rw, TN)[:8]
    in_grad[...] = total.astype(BF)
    router_grad[...] = router[:experts]


def weight_kernel(slots, share, *refs):
    t = lax.axis_index("t")
    near, far, outs, (held, sems) = refs[:5], refs[5:10], refs[10:13], refs[13:]
    copies = []
    for step in range(4):
        rows_of = pl.ds(pl.multiple_of((t ^ step) * share, share), share)
        both = down = 0.0
        for part in (near, far):
            piece, chosen = part[step], part[4]
            both += matmul(piece[:slots, : 2 * share], chosen[:slots], TN)
            down += matmul(piece[:slots, 2 * share :], chosen[slots:], TN)
        for k, value in enumerate((both[:share], both[share:], down)):
            held[k, step] = value.astype(BF)
            copy = pltpu.make_async_copy(held.at[k, step], outs[k].at[rows_of, :], sems.at[k, step])
            copy.start()
            copies.append(copy)
    for copy in copies:
        copy.wait()


def call(body, ins, outs, flops, scratch=(), out_spec=VMEM):
    bytes_moved = sum(v.size * v.dtype.itemsize for v in ins)
    return pl.pallas_call(
        body,
        in_specs=[VMEM] * len(ins),
        out_specs=[out_spec] * len(outs),
        out_shape=[jax.ShapeDtypeStruct(shape, dtype) for shape, dtype in outs],
        scratch_shapes=list(scratch),
        cost_estimate=pl.CostEstimate(
            flops=flops, bytes_accessed=bytes_moved, transcendentals=0
        ),
        compiler_params=pltpu.CompilerParams(vmem_limit_bytes=VMEM_LIMIT),
    )(*ins)


def exchange(value, axis, step):
    count = lax.axis_size(axis)
    return lax.ppermute(value, axis, [(k, k ^ step) for k in range(count)])


def packers():
    per, taken, sent = 2 * CAP, SENT_ROWS, BACK_ROWS
    pack = np.zeros((11, CHIPS, per, CHIPS, taken), np.float32)
    unpack = np.zeros((13, CHIPS, sent, CHIPS * per + 16), np.float32)
    for j in range(CHIPS):
        for k in range(per):
            pack[10, j, k, j, k] = 1.0
            if k < 8:
                unpack[0, j, k, j * per + k] = 1.0
            for kind in range(2):
                if k < 8:
                    pack[5 * kind, j, k, j, 8 * kind + k] = 1.0
                else:
                    for m in range(4):
                        pack[5 * kind + 1 + m, j, k, j, 4 * (k - 8 + 2 * kind) + m] = 1.0
        for i in range(6):
            source = j * per + 8 + i if i < 2 else CHIPS * per + i - 2
            for m in range(4):
                r, c = (4 * i + m) // 3, (4 * i + m) % 3
                unpack[1 + 4 * c + m, j, r, source] = 1.0
    pack = pack.reshape(11 * CHIPS * per, CHIPS * taken)
    unpack = unpack.reshape(13 * CHIPS * sent, CHIPS * per + 16)
    return jnp.asarray(pack, BF), jnp.asarray(unpack, BF)


def shards(stash, out_grad, router_weight, gate_weight, up_weight, down_weight, expert_ids):
    experts, ways = router_weight.shape[0], lax.axis_size("t")
    tokens, width = stash.shape[1], stash.shape[2]
    hidden = gate_weight.shape[0]
    share = hidden // ways
    router_tall = jnp.pad(router_weight, ((0, 128 - experts), (0, 0)))
    packer, unpacker = packers()
    slots = 2 * CHIPS * CAP
    height = slots + 8

    places = 2 * CHIPS
    x_other = lax.ppermute(stash[0], ("p", "c"), [(k, places - 1 - k) for k in range(places)])
    id_columns = jnp.pad(jnp.concatenate([expert_ids[0]] * 2, 0).astype(BF), ((0, 0), (0, 126)))
    block = jnp.concatenate([jnp.concatenate([x_other, out_grad[0]], 0), id_columns], 1)
    (ready,) = call(
        ready_kernel, [x_other, gate_weight, up_weight, down_weight], [((tokens, 128), F32)], 1000
    )
    chosen, own_block = call(
        functools.partial(pick_kernel, width),
        [block, exchange(block, "h", 1), ready],
        [((CHIPS, SENT_ROWS, width + width // 4 + 128), BF), ((2 * tokens, width + 128), BF)],
        8 * width * 32 * SENT_ROWS,
    )
    near = lax.all_to_all(chosen, "p", 0, 0).reshape(CHIPS * SENT_ROWS, -1)
    far = exchange(near, "c", 1)

    halves = []
    for index, block in enumerate((near, far)):
        if index == 1:
            block, _ = lax.optimization_barrier((block, halves[0][2]))
        mine, *sends, taken = call(
            functools.partial(project_kernel, width, share, index == 0),
            [block, gate_weight, up_weight, down_weight, router_tall, packer, own_block],
            [((height, 3 * share + 128), F32)]
            + [((height, 3 * share), BF)] * 3
            + [((2 * slots, width), BF)],
            2 * slots * width * (3 * hidden + 4 * slots),
            [pltpu.VMEM((8, 3 * share), F32)],
        )
        got = [exchange(sends[step - 1], "t", step) for step in (3, 2, 1)]
        halves.append((mine, got, taken))
    gradients = []
    for index, (mine, got, taken) in enumerate(halves):
        packed, weight, local, losses = call(
            functools.partial(act_kernel, width, slots, share, experts, index == 0),
            [own_block, mine, *got],
            [((height, 3 * share), BF), ((slots, 128), F32), ((16, 128), F32), ((1, 2), F32)],
            slots * share * 40,
        )
        pieces = [packed, exchange(packed, "t", 1), exchange(packed, "t", 2)]
        pieces.append(exchange(pieces[2], "t", 1))
        gradients.append((pieces, weight, local, losses))
    _, _, local, losses = gradients[0]

    pieces, weight, _, _ = gradients[0]
    kept, router_near = call(
        functools.partial(near_kernel, width, share),
        [*pieces, gate_weight, up_weight, router_tall, weight, halves[0][2], local, own_block],
        [((slots, width), F32), ((8, width), F32)],
        2 * slots * width * 2 * hidden,
    )
    pieces, weight, _, _ = gradients[1]
    sent, router_part = call(
        functools.partial(far_kernel, share),
        [*pieces, gate_weight, up_weight, router_tall, weight, halves[1][2], router_near],
        [((slots + 16, width), BF), ((8, width), F32)],
        2 * slots * width * 2 * hidden,
    )
    got = exchange(sent, "c", 1)
    (pair,) = call(
        functools.partial(pair_kernel, width),
        [kept, got, router_part, unpacker],
        [((CHIPS * BACK_ROWS, width + 3 * (width // 4)), BF)],
        2 * slots * slots * width,
    )
    got = lax.all_to_all(pair.reshape(CHIPS, BACK_ROWS, -1), "p", 0, 0)
    own_rows, router_part, sent = call(
        functools.partial(group_kernel, width),
        [got],
        [((16, width), F32), ((8, width), F32), ((16, width), BF)],
        slots * width * 2,
    )
    gate_grad, up_grad, down_grad = call(
        functools.partial(weight_kernel, slots, share),
        [*gradients[0][0], halves[0][2], *gradients[1][0], halves[1][2]],
        [((hidden, width), BF)] * 3,
        4 * slots * width * hidden * 3,
        [pltpu.VMEM((3, ways, share, width), BF), pltpu.SemaphoreType.DMA((3, ways))],
        pl.BlockSpec(memory_space=pl.ANY),
    )
    in_grad, router_grad = call(
        functools.partial(final_kernel, width, experts),
        [own_rows, router_part, exchange(sent, "h", 1), own_block, local, router_tall],
        [((tokens, width), BF), ((experts, width), F32)],
        tokens * width * 50,
    )
    return in_grad[None], gate_grad, up_grad, down_grad, router_grad, losses


def solution(mesh):
    ways = mesh.devices.shape[1]
    fine = Mesh(mesh.devices.reshape(2, CHIPS, 2, ways), ("h", "p", "c", "t"))
    section = ("h", "p", "c")
    in_specs = (
        P(section, None, "t"),
        P(section, None, "t"),
        P(None, "t"),
        P(section, "t"),
        P(section, "t"),
        P(section, "t"),
        P(section, None, None),
    )
    out_specs = (
        P(section, None, "t"),
        P(section, "t"),
        P(section, "t"),
        P(section, "t"),
        P(None, "t"),
        P(section, None),
    )
    return jax.shard_map(shards, mesh=fine, in_specs=in_specs, out_specs=out_specs, check_vma=False)
```

```python
import functools

import jax
import jax.numpy as jnp
import numpy as np
from jax import lax
from jax.experimental import pallas as pl
from jax.experimental.pallas import tpu as pltpu
from jax.sharding import Mesh, PartitionSpec as P

CAP = 5
Z_WEIGHT = 0.25
BALANCE_WEIGHT = 1.0
BF = jnp.bfloat16
F32 = jnp.float32
CHIPS = 16
SENT_ROWS = 16
BACK_ROWS = 8
VMEM_LIMIT = 16 * 2**20
VMEM = pl.BlockSpec(memory_space=pltpu.VMEM)
NT = (((1,), (1,)), ((), ()))
TN = (((0,), (0,)), ((), ()))


def matmul(a, b, dims=(((1,), (0,)), ((), ()))):
    return lax.dot_general(a, b, dims, preferred_element_type=F32)


def split_pair(value):
    high = value.astype(BF)
    return high, (value - high.astype(F32)).astype(BF)


def up_to(count, step):
    return -(-count // step) * step


def to_row(value):
    count = value.shape[0]
    padded = up_to(count, 128)
    if padded > count:
        value = jnp.concatenate([value, jnp.zeros((padded - count, 128), F32)], 0)
    return jnp.sum(value.T, axis=0, keepdims=True)


def to_column(row, count):
    padded = up_to(count, 128)
    return jnp.broadcast_to(row[:, :padded], (128, padded)).T[:count]


def row_pair(value, lanes):
    high, low = split_pair(to_row(value))
    rows = jnp.concatenate([high.astype(F32), low.astype(F32), jnp.zeros((6, high.shape[1]), F32)], 0)
    if rows.shape[1] < lanes:
        rows = jnp.concatenate([rows, jnp.zeros((8, lanes - rows.shape[1]), F32)], 1)
    return rows


def spots(ids, expert, row):
    first = jnp.broadcast_to(ids[:, 0:1], ids.shape)
    second = jnp.broadcast_to(ids[:, 1:2], ids.shape)
    match = (first == expert) | (second == expert)
    matched = match.astype(F32)
    position = matched
    for step in (1, 2, 4):
        moved = pltpu.roll(position, step, 0)
        position = position + jnp.where((row & 7) >= step, moved, 0.0)
    return match, position - matched, first + second - expert


def ready_kernel(x, gate_w, up_w, down_w, out):
    out[...] = x[:, :128].astype(F32)


def pick_kernel(width, mine, got, ready, out, own_block):
    first = lax.axis_index("h") * 2
    parts = []
    for x, g in ((got, mine), (mine, got)):
        parts += [jnp.concatenate([x[:8, :width], g[8:, width:]], 1), g[8:, :]]
    blocks = jnp.concatenate(parts, 0)
    own_block[...] = blocks[:16]
    rows, quarter = blocks.shape[0], width // 4
    row = lax.broadcasted_iota(jnp.int32, (rows, 128), 0)
    lane = lax.broadcasted_iota(jnp.int32, (rows, 128), 1).astype(F32)
    grad = ((row & 8) >> 3).astype(F32)
    labels = lax.broadcasted_iota(jnp.int32, (rows, SENT_ROWS), 1).astype(F32)
    ids = blocks[:, width:].astype(F32)

    def pick(label):
        wide = jnp.broadcast_to(label[:, 0:1], (rows, SENT_ROWS))
        return (wide == labels).astype(F32).astype(BF)

    for side in range(2):
        e_value = (first + side).astype(F32)
        match, position, other = spots(ids, e_value, row)
        slot = (row >> 4).astype(F32) * CAP + position
        slot = jnp.where(match, slot, -100.0)
        main = jnp.where(slot < 8, slot + 8.0 * grad, -100.0)
        rest = jnp.where(slot >= 8, (slot - 8.0 + 2.0 * grad) * 4.0, -100.0)
        sign = (lane == e_value).astype(F32) - (lane == other).astype(F32)
        values = matmul(pick(main), blocks[:, :width], TN).astype(BF)
        extra = sum(
            matmul(pick(rest + m), blocks[:, m * quarter : (m + 1) * quarter], TN) for m in range(4)
        ).astype(BF)
        signs = matmul(pick(jnp.where(grad > 0, -100.0, slot)), sign.astype(BF), TN).astype(BF)
        for j in range(side * CHIPS // 2, (side + 1) * CHIPS // 2):
            out[j, :, :width] = values
            out[j, :, width : width + quarter] = extra
            out[j, :, width + quarter :] = signs


def project_kernel(
    width, share, has_own, block, gate_w, up_w, down_w, router_w, packer, own_block,
    own, send1, send2, send3, chosen, notes,
):
    t = lax.axis_index("t")
    slots, quarter = packer.shape[0] // 11, width // 4
    extra = block[:, width : width + quarter]

    def unpack(first):
        parts = []
        for m in range(4):
            taken = matmul(packer[first * slots : (first + 1) * slots, :], block[:, m * quarter : (m + 1) * quarter])
            rows = slice((first + 1 + m) * slots, (first + 2 + m) * slots)
            parts.append((taken + matmul(packer[rows, :], extra)).astype(BF))
        return jnp.concatenate(parts, 1)

    x_slot, g_slot = unpack(0), unpack(5)
    toward = matmul(packer[10 * slots :, :], block[:, width + quarter :])
    chosen[:slots] = x_slot
    chosen[slots:] = g_slot
    lead = matmul(x_slot, router_w[...], NT) * toward
    notes[...] = row_pair(lead, 3 * share)
    if has_own:
        logits = matmul(router_w[:16], own_block[:, :width], NT)[:8]
        high = logits.astype(BF).astype(F32)
        notes[:, 2 * share : 2 * share + 16] = high + pltpu.roll(logits - high, 4, 0)
    own[:slots, 3 * share :] = toward
    own[slots:, 3 * share :] = jnp.zeros((8, 128), F32)
    for step, out in enumerate((own, send1, send2, send3)):
        rows_of = pl.ds(pl.multiple_of((t ^ step) * share, share), share)
        both = jnp.concatenate([gate_w[rows_of, :], up_w[rows_of, :]], 0)
        out[:slots, : 2 * share] = matmul(x_slot, both, NT).astype(out.dtype)
        out[:slots, 2 * share : 3 * share] = matmul(g_slot, down_w[rows_of, :], NT).astype(out.dtype)
        out[slots:, : 3 * share] = notes[...].astype(out.dtype)


def relay_kernel(slots, share, held, got, out):
    total = held[...] + got[...].astype(F32)
    high, low = split_pair(total[slots : slots + 1] + total[slots + 1 : slots + 2])
    zero = jnp.zeros((6, 3 * share), F32)
    notes = jnp.concatenate([high.astype(F32), low.astype(F32), zero], 0)
    out[:slots] = total[:slots].astype(BF)
    out[slots:] = notes.astype(BF)


def act_kernel(width, slots, share, experts, has_own, own_block, own, *refs):
    gots, (packed, weight, local, losses) = refs[:-4], refs[-4:]
    total = own[:, : 3 * share]
    for got in gots:
        total = total + got[...].astype(F32)
    toward = own[:slots, 3 * share :]
    used = jnp.sum(jnp.abs(toward), axis=1, keepdims=True) > 0.5
    lead = to_column(total[slots : slots + 1] + total[slots + 1 : slots + 2], slots)
    w = jnp.where(used, jax.nn.sigmoid(lead), 0.0)
    weight[...] = w * (1.0 - w) * toward
    gate_proj, up_proj, back_proj = (
        total[:slots, k * share : (k + 1) * share] for k in range(3)
    )
    gate_sig = jax.nn.sigmoid(gate_proj)
    silu_gate = gate_proj * gate_sig
    scaled = w * back_proj
    packed[:slots, :share] = (
        scaled * up_proj * gate_sig * (1.0 + gate_proj * (1.0 - gate_sig))
    ).astype(BF)
    packed[:slots, share : 2 * share] = (scaled * silu_gate).astype(BF)
    packed[:slots, 2 * share :] = (w * silu_gate * up_proj).astype(BF)
    rows = row_pair(silu_gate * up_proj * back_proj, 3 * share)
    packed[slots:] = rows.astype(BF)
    if not has_own:
        local[...] = jnp.zeros_like(local)
        losses[...] = jnp.zeros_like(losses)
        return

    logits = total[slots:, 2 * share : 3 * share]
    logits = logits + pltpu.roll(logits, 4, 0)
    expert = lax.broadcasted_iota(jnp.int32, (8, 128), 0)
    real = lax.broadcasted_iota(jnp.int32, (8, 128), 1) < 8
    exp_logits = jnp.where(expert < experts, jnp.exp(logits), 0.0)
    exp_total = jnp.sum(exp_logits, axis=0, keepdims=True)
    log_total = jnp.log(exp_total)
    prob = exp_logits / exp_total
    fraction = jnp.zeros((8, 128), F32)
    ids = own_block[:, width:].astype(F32)[:8]
    for k in range(experts):
        named = (ids[:, 0:1] == k).astype(F32) + (ids[:, 1:2] == k).astype(F32)
        count = jnp.sum(named, axis=0, keepdims=True)
        fraction = jnp.where(expert == k, count / 16.0, fraction)
    pull = BALANCE_WEIGHT * experts * fraction
    inner = jnp.sum(prob * pull, axis=0, keepdims=True)
    rows = 2.0 * Z_WEIGHT * log_total * prob + prob * (pull - inner)
    local[:8] = jnp.where(real, rows, 0.0)
    local[8:] = jnp.zeros((8, 128), F32)
    z_term = jnp.where(real[:1], log_total * log_total, 0.0)
    z_loss = jnp.sum(z_term, axis=1, keepdims=True) / 8.0
    mean_prob = jnp.sum(jnp.where(real, prob, 0.0), axis=1, keepdims=True) / 8.0
    balance = experts * jnp.sum(fraction[:, :1] * mean_prob, axis=0, keepdims=True)
    losses[0:1, 0:1] = z_loss
    losses[0:1, 1:2] = balance


def pair_rows(router):
    high, low = split_pair(router)
    return jnp.concatenate([high.astype(F32), low.astype(F32)], 0).astype(BF)


def slot_gradient(share, pieces, gate_w, up_w, router_w, weight):
    t = lax.axis_index("t")
    slots = weight.shape[0]
    notes = sum(p[slots:, :].astype(F32) for p in pieces)
    high, low = split_pair(to_column(notes[0:1] + notes[1:2], slots) * weight[...])
    total = matmul(high, router_w[...]) + matmul(low, router_w[...])
    for step, piece in enumerate(pieces):
        rows_of = pl.ds(pl.multiple_of((t ^ step) * share, share), share)
        both = jnp.concatenate([gate_w[rows_of, :], up_w[rows_of, :]], 0)
        total += matmul(piece[:slots, : 2 * share], both)
    return total, high, low


def near_kernel(
    width, share, p0, p1, p2, p3, gate_w, up_w, router_w, weight, chosen, local, own_block,
    kept, router_part,
):
    total, high, low = slot_gradient(
        share, (p0, p1, p2, p3), gate_w, up_w, router_w, weight
    )
    slots = total.shape[0]
    kept[...] = total
    x_slot = chosen[:slots]
    router = matmul(high, x_slot, TN)[:8] + matmul(low, x_slot, TN)[:8]
    local_high, local_low = split_pair(local[...])
    router += matmul(local_high[:, :16], own_block[:, :width])[:8]
    router += matmul(local_low[:, :16], own_block[:, :width])[:8]
    router_part[...] = router


def far_kernel(
    share, p0, p1, p2, p3, gate_w, up_w, router_w, weight, chosen, router_near,
    sent, router_part,
):
    total, high, low = slot_gradient(
        share, (p0, p1, p2, p3), gate_w, up_w, router_w, weight
    )
    slots = total.shape[0]
    sent[:slots] = total.astype(BF)
    x_slot = chosen[:slots]
    router = router_near[...]
    router += matmul(high, x_slot, TN)[:8] + matmul(low, x_slot, TN)[:8]
    router_part[...] = router
    sent[slots:] = pair_rows(router)


def pair_kernel(width, kept, got, router_part, unpacker, out):
    half, quarter, count = kept.shape[0], width // 4, out.shape[0]
    pair = (kept[...] + got[:half].astype(F32)).astype(BF)
    rows = got[half:].astype(F32)
    router = (router_part[...] + rows[:8] + rows[8:]).astype(BF).astype(F32)
    router = jnp.concatenate([router, jnp.zeros_like(router)], 0).astype(BF)
    pair = jnp.concatenate([pair, router], 0)
    out[:, :width] = matmul(unpacker[:count, :], pair).astype(BF)
    for c in range(3):
        value = 0.0
        for m in range(4):
            first = (1 + 4 * c + m) * count
            value += matmul(
                unpacker[first : first + count, :], pair[:, m * quarter : (m + 1) * quarter]
            )
        out[:, width + c * quarter : width + (c + 1) * quarter] = value.astype(BF)


def group_kernel(width, got, own, router_part, send):
    quarter = width // 4
    row = lax.broadcasted_iota(jnp.int32, (8, quarter), 0)
    sides = []
    for side in range(2):
        first = side * CHIPS // 2
        total = got[first].astype(F32)
        for j in range(first + 1, first + CHIPS // 2):
            total += got[j].astype(F32)
        more = []
        for m in range(4):
            value = jnp.zeros((8, quarter), F32)
            for i in range(6):
                r, c = (4 * i + m) // 3, (4 * i + m) % 3
                piece = total[r : r + 1, width + c * quarter : width + (c + 1) * quarter]
                value = jnp.where(row == i, jnp.broadcast_to(piece, (8, quarter)), value)
            more.append(value)
        own[8 * side : 8 * side + 8] = total[:, :width]
        sides.append(jnp.concatenate([total[:, :width], jnp.concatenate(more, 1)], 0))
    near, far = sides
    row = lax.broadcasted_iota(jnp.int32, near.shape, 0)
    router_part[...] = pltpu.roll(near + far, 16 - 2 * CAP, 0)[:8]
    send[...] = jnp.where(
        row < CAP, pltpu.roll(near, 16 - CAP, 0), jnp.where(row < 2 * CAP, far, near + far)
    ).astype(BF)


def final_kernel(
    width, experts, own, router_part, got, own_block, local, router_w, in_grad, router_grad
):
    h = lax.axis_index("h")
    ids = own_block[:, width:].astype(F32)[:8]
    row = lax.broadcasted_iota(jnp.int32, (8, 128), 0)
    total = own_block[8:, :width].astype(F32)
    other = got[...].astype(F32)
    router = router_part[...] + pltpu.roll(other, 16 - 2 * CAP, 0)[:8]
    for step in range(2):
        for side in range(2):
            match, position, _ = spots(ids, ((h ^ step) * 2 + side).astype(F32), row)
            for k in range(CAP):
                chosen = (match & (position == k)).astype(F32)[:, 0:1]
                if step == 0:
                    value = own[8 * side + k : 8 * side + k + 1, :]
                else:
                    value = other[CAP * side + k : CAP * side + k + 1]
                total += chosen * value
    high, low = split_pair(local[...])
    rw = router_w[:16]
    total += matmul(high, rw, TN)[:8] + matmul(low, rw, TN)[:8]
    in_grad[...] = total.astype(BF)
    router_grad[...] = router[:experts]


def weight_kernel(slots, share, *refs):
    t = lax.axis_index("t")
    near, far, outs, (held, sems) = refs[:5], refs[5:10], refs[10:13], refs[13:]
    copies = []
    for step in range(4):
        rows_of = pl.ds(pl.multiple_of((t ^ step) * share, share), share)
        both = down = 0.0
        for part in (near, far):
            piece, chosen = part[step], part[4]
            both += matmul(piece[:slots, : 2 * share], chosen[:slots], TN)
            down += matmul(piece[:slots, 2 * share :], chosen[slots:], TN)
        for k, value in enumerate((both[:share], both[share:], down)):
            held[k, step] = value.astype(BF)
            copy = pltpu.make_async_copy(held.at[k, step], outs[k].at[rows_of, :], sems.at[k, step])
            copy.start()
            copies.append(copy)
    for copy in copies:
        copy.wait()


def call(body, ins, outs, flops, scratch=(), out_spec=VMEM):
    bytes_moved = sum(v.size * v.dtype.itemsize for v in ins)
    return pl.pallas_call(
        body,
        in_specs=[VMEM] * len(ins),
        out_specs=[out_spec] * len(outs),
        out_shape=[jax.ShapeDtypeStruct(shape, dtype) for shape, dtype in outs],
        scratch_shapes=list(scratch),
        cost_estimate=pl.CostEstimate(
            flops=flops, bytes_accessed=bytes_moved, transcendentals=0
        ),
        compiler_params=pltpu.CompilerParams(vmem_limit_bytes=VMEM_LIMIT),
    )(*ins)


def exchange(value, axis, step):
    count = lax.axis_size(axis)
    return lax.ppermute(value, axis, [(k, k ^ step) for k in range(count)])


def packers():
    per, taken, sent = 2 * CAP, SENT_ROWS, BACK_ROWS
    pack = np.zeros((11, CHIPS, per, CHIPS, taken), np.float32)
    unpack = np.zeros((13, CHIPS, sent, CHIPS * per + 16), np.float32)
    for j in range(CHIPS):
        for k in range(per):
            pack[10, j, k, j, k] = 1.0
            if k < 8:
                unpack[0, j, k, j * per + k] = 1.0
            for kind in range(2):
                if k < 8:
                    pack[5 * kind, j, k, j, 8 * kind + k] = 1.0
                else:
                    for m in range(4):
                        pack[5 * kind + 1 + m, j, k, j, 4 * (k - 8 + 2 * kind) + m] = 1.0
        for i in range(6):
            source = j * per + 8 + i if i < 2 else CHIPS * per + i - 2
            for m in range(4):
                r, c = (4 * i + m) // 3, (4 * i + m) % 3
                unpack[1 + 4 * c + m, j, r, source] = 1.0
    pack = pack.reshape(11 * CHIPS * per, CHIPS * taken)
    unpack = unpack.reshape(13 * CHIPS * sent, CHIPS * per + 16)
    return jnp.asarray(pack, BF), jnp.asarray(unpack, BF)


def shards(stash, out_grad, router_weight, gate_weight, up_weight, down_weight, expert_ids):
    experts, ways = router_weight.shape[0], lax.axis_size("t")
    tokens, width = stash.shape[1], stash.shape[2]
    hidden = gate_weight.shape[0]
    share = hidden // ways
    router_tall = jnp.pad(router_weight, ((0, 128 - experts), (0, 0)))
    packer, unpacker = packers()
    slots = 2 * CHIPS * CAP
    height = slots + 8

    places = 2 * CHIPS
    x_other = lax.ppermute(stash[0], ("p", "c"), [(k, places - 1 - k) for k in range(places)])
    id_columns = jnp.pad(jnp.concatenate([expert_ids[0]] * 2, 0).astype(BF), ((0, 0), (0, 126)))
    block = jnp.concatenate([jnp.concatenate([x_other, out_grad[0]], 0), id_columns], 1)
    (ready,) = call(
        ready_kernel, [x_other, gate_weight, up_weight, down_weight], [((tokens, 128), F32)], 1000
    )
    chosen, own_block = call(
        functools.partial(pick_kernel, width),
        [block, exchange(block, "h", 1), ready],
        [((CHIPS, SENT_ROWS, width + width // 4 + 128), BF), ((2 * tokens, width + 128), BF)],
        8 * width * 32 * SENT_ROWS,
    )
    near = lax.all_to_all(chosen, "p", 0, 0).reshape(CHIPS * SENT_ROWS, -1)
    far = exchange(near, "c", 1)

    halves = []
    for index, block in enumerate((near, far)):
        if index == 1:
            block, _ = lax.optimization_barrier((block, halves[0][2]))
        mine, *sends, taken = call(
            functools.partial(project_kernel, width, share, index == 0),
            [block, gate_weight, up_weight, down_weight, router_tall, packer, own_block],
            [((height, 3 * share + 128), F32)]
            + [((height, 3 * share), BF), ((height, 3 * share), F32 if index else BF)]
            + [((height, 3 * share), BF), ((2 * slots, width), BF)],
            2 * slots * width * (3 * hidden + 4 * slots),
            [pltpu.VMEM((8, 3 * share), F32)],
        )
        if index == 0:
            got = [exchange(sends[step - 1], "t", step) for step in (3, 2, 1)]
        else:
            passed = exchange(sends[2], "t", 1)
            sends[1], halves[0][1][0] = lax.optimization_barrier((sends[1], halves[0][1][0]))
            (relayed,) = call(
                functools.partial(relay_kernel, slots, share),
                [sends[1], passed],
                [((height, 3 * share), BF)],
                slots * share * 6,
            )
            beside, relayed = lax.optimization_barrier((sends[0], relayed))
            got = [exchange(relayed, "t", 2), exchange(beside, "t", 1)]
        halves.append((mine, got, taken))
    gradients = []
    for index, (mine, got, taken) in enumerate(halves):
        packed, weight, local, losses = call(
            functools.partial(act_kernel, width, slots, share, experts, index == 0),
            [own_block, mine, *got],
            [((height, 3 * share), BF), ((slots, 128), F32), ((16, 128), F32), ((1, 2), F32)],
            slots * share * 40,
        )
        packed_one = packed
        if index == 1:
            packed_one, gradients[0][0][1] = lax.optimization_barrier((packed, gradients[0][0][1]))
        pieces = [packed, exchange(packed_one, "t", 1), exchange(packed, "t", 2)]
        pieces.append(exchange(pieces[2], "t", 1))
        gradients.append((pieces, weight, local, losses))
    _, _, local, losses = gradients[0]

    pieces, weight, _, _ = gradients[0]
    kept, router_near = call(
        functools.partial(near_kernel, width, share),
        [*pieces, gate_weight, up_weight, router_tall, weight, halves[0][2], local, own_block],
        [((slots, width), F32), ((8, width), F32)],
        2 * slots * width * 2 * hidden,
    )
    pieces, weight, _, _ = gradients[1]
    sent, router_part = call(
        functools.partial(far_kernel, share),
        [*pieces, gate_weight, up_weight, router_tall, weight, halves[1][2], router_near],
        [((slots + 16, width), BF), ((8, width), F32)],
        2 * slots * width * 2 * hidden,
    )
    got = exchange(sent, "c", 1)
    (pair,) = call(
        functools.partial(pair_kernel, width),
        [kept, got, router_part, unpacker],
        [((CHIPS * BACK_ROWS, width + 3 * (width // 4)), BF)],
        2 * slots * slots * width,
    )
    got = lax.all_to_all(pair.reshape(CHIPS, BACK_ROWS, -1), "p", 0, 0)
    own_rows, router_part, sent = call(
        functools.partial(group_kernel, width),
        [got],
        [((16, width), F32), ((8, width), F32), ((16, width), BF)],
        slots * width * 2,
    )
    gate_grad, up_grad, down_grad = call(
        functools.partial(weight_kernel, slots, share),
        [*gradients[0][0], halves[0][2], *gradients[1][0], halves[1][2]],
        [((hidden, width), BF)] * 3,
        4 * slots * width * hidden * 3,
        [pltpu.VMEM((3, ways, share, width), BF), pltpu.SemaphoreType.DMA((3, ways))],
        pl.BlockSpec(memory_space=pl.ANY),
    )
    in_grad, router_grad = call(
        functools.partial(final_kernel, width, experts),
        [own_rows, router_part, exchange(sent, "h", 1), own_block, local, router_tall],
        [((tokens, width), BF), ((experts, width), F32)],
        tokens * width * 50,
    )
    return in_grad[None], gate_grad, up_grad, down_grad, router_grad, losses


def solution(mesh):
    ways = mesh.devices.shape[1]
    fine = Mesh(mesh.devices.reshape(2, CHIPS, 2, ways), ("h", "p", "c", "t"))
    section = ("h", "p", "c")
    in_specs = (
        P(section, None, "t"),
        P(section, None, "t"),
        P(None, "t"),
        P(section, "t"),
        P(section, "t"),
        P(section, "t"),
        P(section, None, None),
    )
    out_specs = (
        P(section, None, "t"),
        P(section, "t"),
        P(section, "t"),
        P(section, "t"),
        P(None, "t"),
        P(section, None),
    )
    return jax.shard_map(shards, mesh=fine, in_specs=in_specs, out_specs=out_specs, check_vma=False)
```

```python
import functools

import jax
import jax.numpy as jnp
import numpy as np
from jax import lax
from jax.experimental import pallas as pl
from jax.experimental.pallas import tpu as pltpu
from jax.sharding import Mesh, PartitionSpec as P

CAP = 5
Z_WEIGHT = 0.25
BALANCE_WEIGHT = 1.0
BF = jnp.bfloat16
F32 = jnp.float32
CHIPS = 16
SENT_ROWS = 16
BACK_ROWS = 8
VMEM_LIMIT = 16 * 2**20
VMEM = pl.BlockSpec(memory_space=pltpu.VMEM)
NT = (((1,), (1,)), ((), ()))
TN = (((0,), (0,)), ((), ()))


def matmul(a, b, dims=(((1,), (0,)), ((), ()))):
    return lax.dot_general(a, b, dims, preferred_element_type=F32)


def split_pair(value):
    high = value.astype(BF)
    return high, (value - high.astype(F32)).astype(BF)


def up_to(count, step):
    return -(-count // step) * step


def to_row(value):
    count = value.shape[0]
    padded = up_to(count, 128)
    if padded > count:
        value = jnp.concatenate([value, jnp.zeros((padded - count, 128), F32)], 0)
    return jnp.sum(value.T, axis=0, keepdims=True)


def to_column(row, count):
    padded = up_to(count, 128)
    return jnp.broadcast_to(row[:, :padded], (128, padded)).T[:count]


def row_pair(value, lanes):
    high, low = split_pair(to_row(value))
    rows = jnp.concatenate([high.astype(F32), low.astype(F32), jnp.zeros((6, high.shape[1]), F32)], 0)
    if rows.shape[1] < lanes:
        rows = jnp.concatenate([rows, jnp.zeros((8, lanes - rows.shape[1]), F32)], 1)
    return rows


def spots(ids, expert, row):
    first = jnp.broadcast_to(ids[:, 0:1], ids.shape)
    second = jnp.broadcast_to(ids[:, 1:2], ids.shape)
    match = (first == expert) | (second == expert)
    matched = match.astype(F32)
    position = matched
    for step in (1, 2, 4):
        moved = pltpu.roll(position, step, 0)
        position = position + jnp.where((row & 7) >= step, moved, 0.0)
    return match, position - matched, first + second - expert


def ready_kernel(x, gate_w, up_w, down_w, out):
    out[...] = x[:, :128].astype(F32)


def pick_kernel(width, mine, got, ready, out, own_block):
    first = lax.axis_index("h") * 2
    parts = []
    for x, g in ((got, mine), (mine, got)):
        parts += [jnp.concatenate([x[:8, :width], g[8:, width:]], 1), g[8:, :]]
    blocks = jnp.concatenate(parts, 0)
    own_block[...] = blocks[:16]
    rows, quarter = blocks.shape[0], width // 4
    row = lax.broadcasted_iota(jnp.int32, (rows, 128), 0)
    lane = lax.broadcasted_iota(jnp.int32, (rows, 128), 1).astype(F32)
    grad = ((row & 8) >> 3).astype(F32)
    labels = lax.broadcasted_iota(jnp.int32, (rows, SENT_ROWS), 1).astype(F32)
    ids = blocks[:, width:].astype(F32)

    def pick(label):
        wide = jnp.broadcast_to(label[:, 0:1], (rows, SENT_ROWS))
        return (wide == labels).astype(F32).astype(BF)

    for side in range(2):
        e_value = (first + side).astype(F32)
        match, position, other = spots(ids, e_value, row)
        slot = (row >> 4).astype(F32) * CAP + position
        slot = jnp.where(match, slot, -100.0)
        main = jnp.where(slot < 8, slot + 8.0 * grad, -100.0)
        rest = jnp.where(slot >= 8, (slot - 8.0 + 2.0 * grad) * 4.0, -100.0)
        sign = (lane == e_value).astype(F32) - (lane == other).astype(F32)
        values = matmul(pick(main), blocks[:, :width], TN).astype(BF)
        extra = sum(
            matmul(pick(rest + m), blocks[:, m * quarter : (m + 1) * quarter], TN) for m in range(4)
        ).astype(BF)
        signs = matmul(pick(jnp.where(grad > 0, -100.0, slot)), sign.astype(BF), TN).astype(BF)
        for j in range(side * CHIPS // 2, (side + 1) * CHIPS // 2):
            out[j, :, :width] = values
            out[j, :, width : width + quarter] = extra
            out[j, :, width + quarter :] = signs


def project_kernel(
    width, share, has_own, steps, block, gate_w, up_w, down_w, router_w, packer, own_block,
    *refs,
):
    sends, (own, chosen, notes) = refs[:-3], refs[-3:]
    slots, quarter = packer.shape[0] // 11, width // 4
    extra = block[:, width : width + quarter]

    def unpack(first):
        parts = []
        for m in range(4):
            taken = matmul(packer[first * slots : (first + 1) * slots, :], block[:, m * quarter : (m + 1) * quarter])
            rows = slice((first + 1 + m) * slots, (first + 2 + m) * slots)
            parts.append((taken + matmul(packer[rows, :], extra)).astype(BF))
        return jnp.concatenate(parts, 1)

    x_slot, g_slot = unpack(0), unpack(5)
    toward = matmul(packer[10 * slots :, :], block[:, width + quarter :])
    chosen[:slots] = x_slot
    chosen[slots:] = g_slot
    lead = matmul(x_slot, router_w[...], NT) * toward
    notes[...] = row_pair(lead, 3 * share)
    if has_own:
        logits = matmul(router_w[:16], own_block[:, :width], NT)[:8]
        high = logits.astype(BF).astype(F32)
        notes[:, 2 * share : 2 * share + 16] = high + pltpu.roll(logits - high, 4, 0)
    own[:slots, 3 * share :] = toward
    own[slots:, 3 * share :] = jnp.zeros((8, 128), F32)
    own[slots:, : 3 * share] = notes[...]
    for step, out in zip(steps, sends):
        partial_step(share, step, x_slot, g_slot, gate_w, up_w, down_w, out)
        out[slots:, : 3 * share] = notes[...].astype(out.dtype)
    if len(steps) == 3:
        partial_step(share, 0, x_slot, g_slot, gate_w, up_w, down_w, own)


def partial_step(share, step, x_slot, g_slot, gate_w, up_w, down_w, out):
    t, slots = lax.axis_index("t"), x_slot.shape[0]
    rows_of = pl.ds(pl.multiple_of((t ^ step) * share, share), share)
    both = jnp.concatenate([gate_w[rows_of, :], up_w[rows_of, :]], 0)
    out[:slots, : 2 * share] = matmul(x_slot, both, NT).astype(out.dtype)
    out[:slots, 2 * share : 3 * share] = matmul(g_slot, down_w[rows_of, :], NT).astype(out.dtype)


def rest_kernel(share, begun, chosen, gate_w, up_w, down_w, send2, send1, own):
    slots = chosen.shape[0] // 2
    x_slot, g_slot = chosen[:slots], chosen[slots:]
    own[:slots, 3 * share :] = begun[:slots, 3 * share :]
    own[slots:, :] = begun[slots:, :]
    for step, out in ((2, send2), (1, send1), (0, own)):
        partial_step(share, step, x_slot, g_slot, gate_w, up_w, down_w, out)
        if step:
            out[slots:, :] = begun[slots:, : 3 * share].astype(out.dtype)


def relay_kernel(slots, share, held, got, out):
    total = held[...] + got[...].astype(F32)
    high, low = split_pair(total[slots : slots + 1] + total[slots + 1 : slots + 2])
    zero = jnp.zeros((6, 3 * share), F32)
    notes = jnp.concatenate([high.astype(F32), low.astype(F32), zero], 0)
    out[:slots] = total[:slots].astype(BF)
    out[slots:] = notes.astype(BF)


def act_kernel(width, slots, share, experts, has_own, own_block, own, *refs):
    gots, (packed, weight, local, losses) = refs[:-4], refs[-4:]
    total = own[:, : 3 * share]
    for got in gots:
        total = total + got[...].astype(F32)
    toward = own[:slots, 3 * share :]
    used = jnp.sum(jnp.abs(toward), axis=1, keepdims=True) > 0.5
    lead = to_column(total[slots : slots + 1] + total[slots + 1 : slots + 2], slots)
    w = jnp.where(used, jax.nn.sigmoid(lead), 0.0)
    weight[...] = w * (1.0 - w) * toward
    gate_proj, up_proj, back_proj = (
        total[:slots, k * share : (k + 1) * share] for k in range(3)
    )
    gate_sig = jax.nn.sigmoid(gate_proj)
    silu_gate = gate_proj * gate_sig
    scaled = w * back_proj
    packed[:slots, :share] = (
        scaled * up_proj * gate_sig * (1.0 + gate_proj * (1.0 - gate_sig))
    ).astype(BF)
    packed[:slots, share : 2 * share] = (scaled * silu_gate).astype(BF)
    packed[:slots, 2 * share :] = (w * silu_gate * up_proj).astype(BF)
    rows = row_pair(silu_gate * up_proj * back_proj, 3 * share)
    packed[slots:] = rows.astype(BF)
    if not has_own:
        local[...] = jnp.zeros_like(local)
        losses[...] = jnp.zeros_like(losses)
        return

    logits = total[slots:, 2 * share : 3 * share]
    logits = logits + pltpu.roll(logits, 4, 0)
    expert = lax.broadcasted_iota(jnp.int32, (8, 128), 0)
    real = lax.broadcasted_iota(jnp.int32, (8, 128), 1) < 8
    exp_logits = jnp.where(expert < experts, jnp.exp(logits), 0.0)
    exp_total = jnp.sum(exp_logits, axis=0, keepdims=True)
    log_total = jnp.log(exp_total)
    prob = exp_logits / exp_total
    fraction = jnp.zeros((8, 128), F32)
    ids = own_block[:, width:].astype(F32)[:8]
    for k in range(experts):
        named = (ids[:, 0:1] == k).astype(F32) + (ids[:, 1:2] == k).astype(F32)
        count = jnp.sum(named, axis=0, keepdims=True)
        fraction = jnp.where(expert == k, count / 16.0, fraction)
    pull = BALANCE_WEIGHT * experts * fraction
    inner = jnp.sum(prob * pull, axis=0, keepdims=True)
    rows = 2.0 * Z_WEIGHT * log_total * prob + prob * (pull - inner)
    local[:8] = jnp.where(real, rows, 0.0)
    local[8:] = jnp.zeros((8, 128), F32)
    z_term = jnp.where(real[:1], log_total * log_total, 0.0)
    z_loss = jnp.sum(z_term, axis=1, keepdims=True) / 8.0
    mean_prob = jnp.sum(jnp.where(real, prob, 0.0), axis=1, keepdims=True) / 8.0
    balance = experts * jnp.sum(fraction[:, :1] * mean_prob, axis=0, keepdims=True)
    losses[0:1, 0:1] = z_loss
    losses[0:1, 1:2] = balance


def pair_rows(router):
    high, low = split_pair(router)
    return jnp.concatenate([high.astype(F32), low.astype(F32)], 0).astype(BF)


def slot_gradient(share, pieces, gate_w, up_w, router_w, weight):
    t = lax.axis_index("t")
    slots = weight.shape[0]
    notes = sum(p[slots:, :].astype(F32) for p in pieces)
    high, low = split_pair(to_column(notes[0:1] + notes[1:2], slots) * weight[...])
    total = matmul(high, router_w[...]) + matmul(low, router_w[...])
    for step, piece in enumerate(pieces):
        rows_of = pl.ds(pl.multiple_of((t ^ step) * share, share), share)
        both = jnp.concatenate([gate_w[rows_of, :], up_w[rows_of, :]], 0)
        total += matmul(piece[:slots, : 2 * share], both)
    return total, high, low


def near_kernel(
    width, share, p0, p1, p2, p3, gate_w, up_w, router_w, weight, chosen, local, own_block,
    kept, router_part,
):
    total, high, low = slot_gradient(
        share, (p0, p1, p2, p3), gate_w, up_w, router_w, weight
    )
    slots = total.shape[0]
    kept[...] = total
    x_slot = chosen[:slots]
    router = matmul(high, x_slot, TN)[:8] + matmul(low, x_slot, TN)[:8]
    local_high, local_low = split_pair(local[...])
    router += matmul(local_high[:, :16], own_block[:, :width])[:8]
    router += matmul(local_low[:, :16], own_block[:, :width])[:8]
    router_part[...] = router


def far_kernel(
    share, p0, p1, p2, p3, gate_w, up_w, router_w, weight, chosen, router_near,
    sent, router_part,
):
    total, high, low = slot_gradient(
        share, (p0, p1, p2, p3), gate_w, up_w, router_w, weight
    )
    slots = total.shape[0]
    sent[:slots] = total.astype(BF)
    x_slot = chosen[:slots]
    router = router_near[...]
    router += matmul(high, x_slot, TN)[:8] + matmul(low, x_slot, TN)[:8]
    router_part[...] = router
    sent[slots:] = pair_rows(router)


def pair_kernel(width, kept, got, router_part, unpacker, out):
    half, quarter, count = kept.shape[0], width // 4, out.shape[0]
    pair = (kept[...] + got[:half].astype(F32)).astype(BF)
    rows = got[half:].astype(F32)
    router = (router_part[...] + rows[:8] + rows[8:]).astype(BF).astype(F32)
    router = jnp.concatenate([router, jnp.zeros_like(router)], 0).astype(BF)
    pair = jnp.concatenate([pair, router], 0)
    out[:, :width] = matmul(unpacker[:count, :], pair).astype(BF)
    for c in range(3):
        value = 0.0
        for m in range(4):
            first = (1 + 4 * c + m) * count
            value += matmul(
                unpacker[first : first + count, :], pair[:, m * quarter : (m + 1) * quarter]
            )
        out[:, width + c * quarter : width + (c + 1) * quarter] = value.astype(BF)


def group_kernel(width, got, own, router_part, send):
    quarter = width // 4
    row = lax.broadcasted_iota(jnp.int32, (8, quarter), 0)
    sides = []
    for side in range(2):
        first = side * CHIPS // 2
        total = got[first].astype(F32)
        for j in range(first + 1, first + CHIPS // 2):
            total += got[j].astype(F32)
        more = []
        for m in range(4):
            value = jnp.zeros((8, quarter), F32)
            for i in range(6):
                r, c = (4 * i + m) // 3, (4 * i + m) % 3
                piece = total[r : r + 1, width + c * quarter : width + (c + 1) * quarter]
                value = jnp.where(row == i, jnp.broadcast_to(piece, (8, quarter)), value)
            more.append(value)
        own[8 * side : 8 * side + 8] = total[:, :width]
        sides.append(jnp.concatenate([total[:, :width], jnp.concatenate(more, 1)], 0))
    near, far = sides
    row = lax.broadcasted_iota(jnp.int32, near.shape, 0)
    router_part[...] = pltpu.roll(near + far, 16 - 2 * CAP, 0)[:8]
    send[...] = jnp.where(
        row < CAP, pltpu.roll(near, 16 - CAP, 0), jnp.where(row < 2 * CAP, far, near + far)
    ).astype(BF)


def final_kernel(
    width, experts, own, router_part, got, own_block, local, router_w, in_grad, router_grad
):
    h = lax.axis_index("h")
    ids = own_block[:, width:].astype(F32)[:8]
    row = lax.broadcasted_iota(jnp.int32, (8, 128), 0)
    total = own_block[8:, :width].astype(F32)
    other = got[...].astype(F32)
    router = router_part[...] + pltpu.roll(other, 16 - 2 * CAP, 0)[:8]
    for step in range(2):
        for side in range(2):
            match, position, _ = spots(ids, ((h ^ step) * 2 + side).astype(F32), row)
            for k in range(CAP):
                chosen = (match & (position == k)).astype(F32)[:, 0:1]
                if step == 0:
                    value = own[8 * side + k : 8 * side + k + 1, :]
                else:
                    value = other[CAP * side + k : CAP * side + k + 1]
                total += chosen * value
    high, low = split_pair(local[...])
    rw = router_w[:16]
    total += matmul(high, rw, TN)[:8] + matmul(low, rw, TN)[:8]
    in_grad[...] = total.astype(BF)
    router_grad[...] = router[:experts]


def weight_kernel(slots, share, *refs):
    t = lax.axis_index("t")
    near, far, outs, (held, sems) = refs[:5], refs[5:10], refs[10:13], refs[13:]
    copies = []
    for step in range(4):
        rows_of = pl.ds(pl.multiple_of((t ^ step) * share, share), share)
        both = down = 0.0
        for part in (near, far):
            piece, chosen = part[step], part[4]
            both += matmul(piece[:slots, : 2 * share], chosen[:slots], TN)
            down += matmul(piece[:slots, 2 * share :], chosen[slots:], TN)
        for k, value in enumerate((both[:share], both[share:], down)):
            held[k, step] = value.astype(BF)
            copy = pltpu.make_async_copy(held.at[k, step], outs[k].at[rows_of, :], sems.at[k, step])
            copy.start()
            copies.append(copy)
    for copy in copies:
        copy.wait()


def call(body, ins, outs, flops, scratch=(), out_spec=VMEM):
    bytes_moved = sum(v.size * v.dtype.itemsize for v in ins)
    return pl.pallas_call(
        body,
        in_specs=[VMEM] * len(ins),
        out_specs=[out_spec] * len(outs),
        out_shape=[jax.ShapeDtypeStruct(shape, dtype) for shape, dtype in outs],
        scratch_shapes=list(scratch),
        cost_estimate=pl.CostEstimate(
            flops=flops, bytes_accessed=bytes_moved, transcendentals=0
        ),
        compiler_params=pltpu.CompilerParams(vmem_limit_bytes=VMEM_LIMIT),
    )(*ins)


def exchange(value, axis, step):
    count = lax.axis_size(axis)
    return lax.ppermute(value, axis, [(k, k ^ step) for k in range(count)])


def packers():
    per, taken, sent = 2 * CAP, SENT_ROWS, BACK_ROWS
    pack = np.zeros((11, CHIPS, per, CHIPS, taken), np.float32)
    unpack = np.zeros((13, CHIPS, sent, CHIPS * per + 16), np.float32)
    for j in range(CHIPS):
        for k in range(per):
            pack[10, j, k, j, k] = 1.0
            if k < 8:
                unpack[0, j, k, j * per + k] = 1.0
            for kind in range(2):
                if k < 8:
                    pack[5 * kind, j, k, j, 8 * kind + k] = 1.0
                else:
                    for m in range(4):
                        pack[5 * kind + 1 + m, j, k, j, 4 * (k - 8 + 2 * kind) + m] = 1.0
        for i in range(6):
            source = j * per + 8 + i if i < 2 else CHIPS * per + i - 2
            for m in range(4):
                r, c = (4 * i + m) // 3, (4 * i + m) % 3
                unpack[1 + 4 * c + m, j, r, source] = 1.0
    pack = pack.reshape(11 * CHIPS * per, CHIPS * taken)
    unpack = unpack.reshape(13 * CHIPS * sent, CHIPS * per + 16)
    return jnp.asarray(pack, BF), jnp.asarray(unpack, BF)


def shards(stash, out_grad, router_weight, gate_weight, up_weight, down_weight, expert_ids):
    experts, ways = router_weight.shape[0], lax.axis_size("t")
    tokens, width = stash.shape[1], stash.shape[2]
    hidden = gate_weight.shape[0]
    share = hidden // ways
    router_tall = jnp.pad(router_weight, ((0, 128 - experts), (0, 0)))
    packer, unpacker = packers()
    slots = 2 * CHIPS * CAP
    height = slots + 8

    places = 2 * CHIPS
    x_other = lax.ppermute(stash[0], ("p", "c"), [(k, places - 1 - k) for k in range(places)])
    id_columns = jnp.pad(jnp.concatenate([expert_ids[0]] * 2, 0).astype(BF), ((0, 0), (0, 126)))
    block = jnp.concatenate([jnp.concatenate([x_other, out_grad[0]], 0), id_columns], 1)
    (ready,) = call(
        ready_kernel, [x_other, gate_weight, up_weight, down_weight], [((tokens, 128), F32)], 1000
    )
    chosen, own_block = call(
        functools.partial(pick_kernel, width),
        [block, exchange(block, "h", 1), ready],
        [((CHIPS, SENT_ROWS, width + width // 4 + 128), BF), ((2 * tokens, width + 128), BF)],
        8 * width * 32 * SENT_ROWS,
    )
    near = lax.all_to_all(chosen, "p", 0, 0).reshape(CHIPS * SENT_ROWS, -1)
    far = exchange(near, "c", 1)

    halves = []
    for index, block in enumerate((near, far)):
        if index == 1:
            block, _ = lax.optimization_barrier((block, halves[0][0]))
        steps = (1, 2, 3) if index else (3,)
        types = (BF, F32, BF) if index else (BF,)
        *sends, mine, taken = call(
            functools.partial(project_kernel, width, share, index == 0, steps),
            [block, gate_weight, up_weight, down_weight, router_tall, packer, own_block],
            [((height, 3 * share), dtype) for dtype in types]
            + [((height, 3 * share + 128), F32), ((2 * slots, width), BF)],
            2 * slots * width * (3 * share * len(steps) + 4 * slots),
            [pltpu.VMEM((8, 3 * share), F32)],
        )
        if index == 0:
            later = call(
                functools.partial(rest_kernel, share),
                [mine, taken, gate_weight, up_weight, down_weight],
                [((height, 3 * share), BF)] * 2 + [((height, 3 * share + 128), F32)],
                2 * slots * width * 9 * share,
            )
            sends, mine = [later[1], later[0], sends[0]], later[2]
        if index == 0:
            got = [exchange(sends[step - 1], "t", step) for step in (3, 2, 1)]
        else:
            passed = exchange(sends[2], "t", 1)
            sends[1], halves[0][1][0] = lax.optimization_barrier((sends[1], halves[0][1][0]))
            (relayed,) = call(
                functools.partial(relay_kernel, slots, share),
                [sends[1], passed],
                [((height, 3 * share), BF)],
                slots * share * 6,
            )
            beside, relayed = lax.optimization_barrier((sends[0], relayed))
            got = [exchange(relayed, "t", 2), exchange(beside, "t", 1)]
        halves.append((mine, got, taken))
    gradients = []
    for index, (mine, got, taken) in enumerate(halves):
        packed, weight, local, losses = call(
            functools.partial(act_kernel, width, slots, share, experts, index == 0),
            [own_block, mine, *got],
            [((height, 3 * share), BF), ((slots, 128), F32), ((16, 128), F32), ((1, 2), F32)],
            slots * share * 40,
        )
        packed_one = packed
        if index == 1:
            packed_one, gradients[0][0][1] = lax.optimization_barrier((packed, gradients[0][0][1]))
        pieces = [packed, exchange(packed_one, "t", 1), exchange(packed, "t", 2)]
        pieces.append(exchange(pieces[2], "t", 1))
        gradients.append((pieces, weight, local, losses))
    _, _, local, losses = gradients[0]

    pieces, weight, _, _ = gradients[0]
    kept, router_near = call(
        functools.partial(near_kernel, width, share),
        [*pieces, gate_weight, up_weight, router_tall, weight, halves[0][2], local, own_block],
        [((slots, width), F32), ((8, width), F32)],
        2 * slots * width * 2 * hidden,
    )
    pieces, weight, _, _ = gradients[1]
    sent, router_part = call(
        functools.partial(far_kernel, share),
        [*pieces, gate_weight, up_weight, router_tall, weight, halves[1][2], router_near],
        [((slots + 16, width), BF), ((8, width), F32)],
        2 * slots * width * 2 * hidden,
    )
    got = exchange(sent, "c", 1)
    (pair,) = call(
        functools.partial(pair_kernel, width),
        [kept, got, router_part, unpacker],
        [((CHIPS * BACK_ROWS, width + 3 * (width // 4)), BF)],
        2 * slots * slots * width,
    )
    got = lax.all_to_all(pair.reshape(CHIPS, BACK_ROWS, -1), "p", 0, 0)
    own_rows, router_part, sent = call(
        functools.partial(group_kernel, width),
        [got],
        [((16, width), F32), ((8, width), F32), ((16, width), BF)],
        slots * width * 2,
    )
    gate_grad, up_grad, down_grad = call(
        functools.partial(weight_kernel, slots, share),
        [*gradients[0][0], halves[0][2], *gradients[1][0], halves[1][2]],
        [((hidden, width), BF)] * 3,
        4 * slots * width * hidden * 3,
        [pltpu.VMEM((3, ways, share, width), BF), pltpu.SemaphoreType.DMA((3, ways))],
        pl.BlockSpec(memory_space=pl.ANY),
    )
    in_grad, router_grad = call(
        functools.partial(final_kernel, width, experts),
        [own_rows, router_part, exchange(sent, "h", 1), own_block, local, router_tall],
        [((tokens, width), BF), ((experts, width), F32)],
        tokens * width * 50,
    )
    return in_grad[None], gate_grad, up_grad, down_grad, router_grad, losses


def solution(mesh):
    ways = mesh.devices.shape[1]
    fine = Mesh(mesh.devices.reshape(2, CHIPS, 2, ways), ("h", "p", "c", "t"))
    section = ("h", "p", "c")
    in_specs = (
        P(section, None, "t"),
        P(section, None, "t"),
        P(None, "t"),
        P(section, "t"),
        P(section, "t"),
        P(section, "t"),
        P(section, None, None),
    )
    out_specs = (
        P(section, None, "t"),
        P(section, "t"),
        P(section, "t"),
        P(section, "t"),
        P(None, "t"),
        P(section, None),
    )
    return jax.shard_map(shards, mesh=fine, in_specs=in_specs, out_specs=out_specs, check_vma=False)
```

```python
import functools

import jax
import jax.numpy as jnp
import numpy as np
from jax import lax
from jax.experimental import pallas as pl
from jax.experimental.pallas import tpu as pltpu
from jax.sharding import Mesh, PartitionSpec as P

CAP = 5
Z_WEIGHT = 0.25
BALANCE_WEIGHT = 1.0
BF = jnp.bfloat16
F32 = jnp.float32
CHIPS = 16
SENT_ROWS = 16
BACK_ROWS = 8
VMEM_LIMIT = 16 * 2**20
VMEM = pl.BlockSpec(memory_space=pltpu.VMEM)
NT = (((1,), (1,)), ((), ()))
TN = (((0,), (0,)), ((), ()))


def matmul(a, b, dims=(((1,), (0,)), ((), ()))):
    return lax.dot_general(a, b, dims, preferred_element_type=F32)


def split_pair(value):
    high = value.astype(BF)
    return high, (value - high.astype(F32)).astype(BF)


def up_to(count, step):
    return -(-count // step) * step


def to_row(value):
    count = value.shape[0]
    padded = up_to(count, 128)
    if padded > count:
        value = jnp.concatenate([value, jnp.zeros((padded - count, 128), F32)], 0)
    return jnp.sum(value.T, axis=0, keepdims=True)


def to_column(row, count):
    padded = up_to(count, 128)
    return jnp.broadcast_to(row[:, :padded], (128, padded)).T[:count]


def row_pair(value, lanes):
    high, low = split_pair(to_row(value))
    rows = jnp.concatenate([high.astype(F32), low.astype(F32), jnp.zeros((6, high.shape[1]), F32)], 0)
    if rows.shape[1] < lanes:
        rows = jnp.concatenate([rows, jnp.zeros((8, lanes - rows.shape[1]), F32)], 1)
    return rows


def spots(ids, expert, row):
    first = jnp.broadcast_to(ids[:, 0:1], ids.shape)
    second = jnp.broadcast_to(ids[:, 1:2], ids.shape)
    match = (first == expert) | (second == expert)
    matched = match.astype(F32)
    position = matched
    for step in (1, 2, 4):
        moved = pltpu.roll(position, step, 0)
        position = position + jnp.where((row & 7) >= step, moved, 0.0)
    return match, position - matched, first + second - expert


def ready_kernel(x, gate_w, up_w, down_w, out):
    out[...] = x[:, :128].astype(F32)


def pick_kernel(width, mine, got, ready, out, own_block):
    first = lax.axis_index("h") * 2
    parts = []
    for x, g in ((got, mine), (mine, got)):
        parts += [jnp.concatenate([x[:8, :width], g[8:, width:]], 1), g[8:, :]]
    blocks = jnp.concatenate(parts, 0)
    own_block[...] = blocks[:16]
    rows, quarter = blocks.shape[0], width // 4
    row = lax.broadcasted_iota(jnp.int32, (rows, 128), 0)
    lane = lax.broadcasted_iota(jnp.int32, (rows, 128), 1).astype(F32)
    grad = ((row & 8) >> 3).astype(F32)
    labels = lax.broadcasted_iota(jnp.int32, (rows, SENT_ROWS), 1).astype(F32)
    ids = blocks[:, width:].astype(F32)

    def pick(label):
        wide = jnp.broadcast_to(label[:, 0:1], (rows, SENT_ROWS))
        return (wide == labels).astype(F32).astype(BF)

    for side in range(2):
        e_value = (first + side).astype(F32)
        match, position, other = spots(ids, e_value, row)
        slot = (row >> 4).astype(F32) * CAP + position
        slot = jnp.where(match, slot, -100.0)
        main = jnp.where(slot < 8, slot + 8.0 * grad, -100.0)
        rest = jnp.where(slot >= 8, (slot - 8.0 + 2.0 * grad) * 4.0, -100.0)
        sign = (lane == e_value).astype(F32) - (lane == other).astype(F32)
        values = matmul(pick(main), blocks[:, :width], TN).astype(BF)
        extra = sum(
            matmul(pick(rest + m), blocks[:, m * quarter : (m + 1) * quarter], TN) for m in range(4)
        ).astype(BF)
        signs = matmul(pick(jnp.where(grad > 0, -100.0, slot)), sign.astype(BF), TN).astype(BF)
        for j in range(side * CHIPS // 2, (side + 1) * CHIPS // 2):
            out[j, :, :width] = values
            out[j, :, width : width + quarter] = extra
            out[j, :, width + quarter :] = signs


def project_kernel(
    width, share, has_own, steps, block, gate_w, up_w, down_w, router_w, packer, own_block,
    *refs,
):
    sends, (own, chosen, notes) = refs[:-3], refs[-3:]
    slots, quarter = packer.shape[0] // 11, width // 4
    extra = block[:, width : width + quarter]

    def unpack(first):
        parts = []
        for m in range(4):
            taken = matmul(packer[first * slots : (first + 1) * slots, :], block[:, m * quarter : (m + 1) * quarter])
            rows = slice((first + 1 + m) * slots, (first + 2 + m) * slots)
            parts.append((taken + matmul(packer[rows, :], extra)).astype(BF))
        return jnp.concatenate(parts, 1)

    x_slot, g_slot = unpack(0), unpack(5)
    toward = matmul(packer[10 * slots :, :], block[:, width + quarter :])
    chosen[:slots] = x_slot
    chosen[slots:] = g_slot
    lead = matmul(x_slot, router_w[...], NT) * toward
    notes[...] = row_pair(lead, 3 * share)
    if has_own:
        logits = matmul(router_w[:16], own_block[:, :width], NT)[:8]
        high = logits.astype(BF).astype(F32)
        notes[:, 2 * share : 2 * share + 16] = high + pltpu.roll(logits - high, 4, 0)
    own[:slots, 3 * share :] = toward
    own[slots:, 3 * share :] = jnp.zeros((8, 128), F32)
    own[slots:, : 3 * share] = notes[...]
    for step, out in zip(steps, sends):
        partial_step(share, step, x_slot, g_slot, gate_w, up_w, down_w, out)
        out[slots:, : 3 * share] = notes[...].astype(out.dtype)
    if len(steps) == 3:
        partial_step(share, 0, x_slot, g_slot, gate_w, up_w, down_w, own)


def partial_step(share, step, x_slot, g_slot, gate_w, up_w, down_w, out):
    t, slots = lax.axis_index("t"), x_slot.shape[0]
    rows_of = pl.ds(pl.multiple_of((t ^ step) * share, share), share)
    both = jnp.concatenate([gate_w[rows_of, :], up_w[rows_of, :]], 0)
    out[:slots, : 2 * share] = matmul(x_slot, both, NT).astype(out.dtype)
    out[:slots, 2 * share : 3 * share] = matmul(g_slot, down_w[rows_of, :], NT).astype(out.dtype)


def rest_kernel(share, begun, chosen, gate_w, up_w, down_w, send2, send1, own):
    slots = chosen.shape[0] // 2
    x_slot, g_slot = chosen[:slots], chosen[slots:]
    own[:slots, 3 * share :] = begun[:slots, 3 * share :]
    own[slots:, :] = begun[slots:, :]
    for step, out in ((2, send2), (1, send1), (0, own)):
        partial_step(share, step, x_slot, g_slot, gate_w, up_w, down_w, out)
        if step:
            out[slots:, :] = begun[slots:, : 3 * share].astype(out.dtype)


def relay_kernel(slots, share, held, got, out):
    total = held[...] + got[...].astype(F32)
    high, low = split_pair(total[slots : slots + 1] + total[slots + 1 : slots + 2])
    zero = jnp.zeros((6, 3 * share), F32)
    notes = jnp.concatenate([high.astype(F32), low.astype(F32), zero], 0)
    out[:slots] = total[:slots].astype(BF)
    out[slots:] = notes.astype(BF)


def act_kernel(width, slots, share, experts, has_own, own_block, own, *refs):
    gots, (packed, weight, local, losses) = refs[:-4], refs[-4:]
    total = own[:, : 3 * share]
    for got in gots:
        total = total + got[...].astype(F32)
    toward = own[:slots, 3 * share :]
    used = jnp.sum(jnp.abs(toward), axis=1, keepdims=True) > 0.5
    lead = to_column(total[slots : slots + 1] + total[slots + 1 : slots + 2], slots)
    w = jnp.where(used, jax.nn.sigmoid(lead), 0.0)
    weight[...] = w * (1.0 - w) * toward
    gate_proj, up_proj, back_proj = (
        total[:slots, k * share : (k + 1) * share] for k in range(3)
    )
    gate_sig = jax.nn.sigmoid(gate_proj)
    silu_gate = gate_proj * gate_sig
    scaled = w * back_proj
    packed[:slots, :share] = (
        scaled * up_proj * gate_sig * (1.0 + gate_proj * (1.0 - gate_sig))
    ).astype(BF)
    packed[:slots, share : 2 * share] = (scaled * silu_gate).astype(BF)
    packed[:slots, 2 * share :] = (w * silu_gate * up_proj).astype(BF)
    rows = row_pair(silu_gate * up_proj * back_proj, 3 * share)
    packed[slots:] = rows.astype(BF)
    if not has_own:
        local[...] = jnp.zeros_like(local)
        losses[...] = jnp.zeros_like(losses)
        return

    logits = total[slots:, 2 * share : 3 * share]
    logits = logits + pltpu.roll(logits, 4, 0)
    expert = lax.broadcasted_iota(jnp.int32, (8, 128), 0)
    real = lax.broadcasted_iota(jnp.int32, (8, 128), 1) < 8
    exp_logits = jnp.where(expert < experts, jnp.exp(logits), 0.0)
    exp_total = jnp.sum(exp_logits, axis=0, keepdims=True)
    log_total = jnp.log(exp_total)
    prob = exp_logits / exp_total
    fraction = jnp.zeros((8, 128), F32)
    ids = own_block[:, width:].astype(F32)[:8]
    for k in range(experts):
        named = (ids[:, 0:1] == k).astype(F32) + (ids[:, 1:2] == k).astype(F32)
        count = jnp.sum(named, axis=0, keepdims=True)
        fraction = jnp.where(expert == k, count / 16.0, fraction)
    pull = BALANCE_WEIGHT * experts * fraction
    inner = jnp.sum(prob * pull, axis=0, keepdims=True)
    rows = 2.0 * Z_WEIGHT * log_total * prob + prob * (pull - inner)
    local[:8] = jnp.where(real, rows, 0.0)
    local[8:] = jnp.zeros((8, 128), F32)
    z_term = jnp.where(real[:1], log_total * log_total, 0.0)
    z_loss = jnp.sum(z_term, axis=1, keepdims=True) / 8.0
    mean_prob = jnp.sum(jnp.where(real, prob, 0.0), axis=1, keepdims=True) / 8.0
    balance = experts * jnp.sum(fraction[:, :1] * mean_prob, axis=0, keepdims=True)
    losses[0:1, 0:1] = z_loss
    losses[0:1, 1:2] = balance


def pair_rows(router):
    high, low = split_pair(router)
    return jnp.concatenate([high.astype(F32), low.astype(F32)], 0).astype(BF)


def slot_gradient(share, pieces, gate_w, up_w, router_w, weight):
    t = lax.axis_index("t")
    slots = weight.shape[0]
    notes = sum(p[slots:, :].astype(F32) for p in pieces)
    high, low = split_pair(to_column(notes[0:1] + notes[1:2], slots) * weight[...])
    total = matmul(high, router_w[...]) + matmul(low, router_w[...])
    for step, piece in enumerate(pieces):
        rows_of = pl.ds(pl.multiple_of((t ^ step) * share, share), share)
        both = jnp.concatenate([gate_w[rows_of, :], up_w[rows_of, :]], 0)
        total += matmul(piece[:slots, : 2 * share], both)
    return total, high, low


def near_kernel(
    width, share, p0, p1, p2, p3, gate_w, up_w, router_w, weight, chosen, local, own_block,
    kept, router_part,
):
    total, high, low = slot_gradient(
        share, (p0, p1, p2, p3), gate_w, up_w, router_w, weight
    )
    slots = total.shape[0]
    kept[...] = total
    x_slot = chosen[:slots]
    router = matmul(high, x_slot, TN)[:8] + matmul(low, x_slot, TN)[:8]
    local_high, local_low = split_pair(local[...])
    router += matmul(local_high[:, :16], own_block[:, :width])[:8]
    router += matmul(local_low[:, :16], own_block[:, :width])[:8]
    router_part[...] = router


def far_kernel(
    share, p0, p1, p2, p3, gate_w, up_w, router_w, weight, chosen, router_near,
    sent, router_part,
):
    total, high, low = slot_gradient(
        share, (p0, p1, p2, p3), gate_w, up_w, router_w, weight
    )
    slots = total.shape[0]
    sent[:slots] = total.astype(BF)
    x_slot = chosen[:slots]
    router = router_near[...]
    router += matmul(high, x_slot, TN)[:8] + matmul(low, x_slot, TN)[:8]
    router_part[...] = router
    sent[slots:] = pair_rows(router)


def pair_kernel(width, kept, got, router_part, unpacker, out):
    half, quarter, count = kept.shape[0], width // 4, out.shape[0]
    pair = (kept[...] + got[:half].astype(F32)).astype(BF)
    rows = got[half:].astype(F32)
    router = (router_part[...] + rows[:8] + rows[8:]).astype(BF).astype(F32)
    router = jnp.concatenate([router, jnp.zeros_like(router)], 0).astype(BF)
    pair = jnp.concatenate([pair, router], 0)
    out[:, :width] = matmul(unpacker[:count, :], pair).astype(BF)
    for c in range(3):
        value = 0.0
        for m in range(4):
            first = (1 + 4 * c + m) * count
            value += matmul(
                unpacker[first : first + count, :], pair[:, m * quarter : (m + 1) * quarter]
            )
        out[:, width + c * quarter : width + (c + 1) * quarter] = value.astype(BF)


def group_kernel(width, got, own, router_part, send):
    quarter = width // 4
    row = lax.broadcasted_iota(jnp.int32, (8, quarter), 0)
    sides = []
    for side in range(2):
        first = side * CHIPS // 2
        total = got[first].astype(F32)
        for j in range(first + 1, first + CHIPS // 2):
            total += got[j].astype(F32)
        more = []
        for m in range(4):
            value = jnp.zeros((8, quarter), F32)
            for i in range(6):
                r, c = (4 * i + m) // 3, (4 * i + m) % 3
                piece = total[r : r + 1, width + c * quarter : width + (c + 1) * quarter]
                value = jnp.where(row == i, jnp.broadcast_to(piece, (8, quarter)), value)
            more.append(value)
        own[8 * side : 8 * side + 8] = total[:, :width]
        sides.append(jnp.concatenate([total[:, :width], jnp.concatenate(more, 1)], 0))
    near, far = sides
    row = lax.broadcasted_iota(jnp.int32, near.shape, 0)
    router_part[...] = pltpu.roll(near + far, 16 - 2 * CAP, 0)[:8]
    send[...] = jnp.where(
        row < CAP, pltpu.roll(near, 16 - CAP, 0), jnp.where(row < 2 * CAP, far, near + far)
    ).astype(BF)


def chosen_rows(ids, half, rows, stride):
    row = lax.broadcasted_iota(jnp.int32, (8, 128), 0)
    total = 0.0
    for side in range(2):
        match, position, _ = spots(ids, (half * 2 + side).astype(F32), row)
        for k in range(CAP):
            chosen = (match & (position == k)).astype(F32)[:, 0:1]
            total += chosen * rows[stride * side + k : stride * side + k + 1]
    return total


def base_kernel(width, own, own_block, local, router_w, base):
    ids = own_block[:, width:].astype(F32)[:8]
    total = own_block[8:, :width].astype(F32)
    total += chosen_rows(ids, lax.axis_index("h"), own[...], 8)
    high, low = split_pair(local[...])
    rw = router_w[:16]
    base[...] = total + matmul(high, rw, TN)[:8] + matmul(low, rw, TN)[:8]


def final_kernel(width, experts, base, router_part, got, own_block, in_grad, router_grad):
    ids = own_block[:, width:].astype(F32)[:8]
    other = got[...].astype(F32)
    router = router_part[...] + pltpu.roll(other, 16 - 2 * CAP, 0)[:8]
    total = base[...] + chosen_rows(ids, lax.axis_index("h") ^ 1, other, CAP)
    in_grad[...] = total.astype(BF)
    router_grad[...] = router[:experts]


def weight_kernel(slots, share, *refs):
    t = lax.axis_index("t")
    near, far, outs, (held, sems) = refs[:5], refs[5:10], refs[10:13], refs[13:]
    copies = []
    for step in range(4):
        rows_of = pl.ds(pl.multiple_of((t ^ step) * share, share), share)
        both = down = 0.0
        for part in (near, far):
            piece, chosen = part[step], part[4]
            both += matmul(piece[:slots, : 2 * share], chosen[:slots], TN)
            down += matmul(piece[:slots, 2 * share :], chosen[slots:], TN)
        for k, value in enumerate((both[:share], both[share:], down)):
            held[k, step] = value.astype(BF)
            copy = pltpu.make_async_copy(held.at[k, step], outs[k].at[rows_of, :], sems.at[k, step])
            copy.start()
            copies.append(copy)
    for copy in copies:
        copy.wait()


def call(body, ins, outs, flops, scratch=(), out_spec=VMEM):
    bytes_moved = sum(v.size * v.dtype.itemsize for v in ins)
    return pl.pallas_call(
        body,
        in_specs=[VMEM] * len(ins),
        out_specs=[out_spec] * len(outs),
        out_shape=[jax.ShapeDtypeStruct(shape, dtype) for shape, dtype in outs],
        scratch_shapes=list(scratch),
        cost_estimate=pl.CostEstimate(
            flops=flops, bytes_accessed=bytes_moved, transcendentals=0
        ),
        compiler_params=pltpu.CompilerParams(vmem_limit_bytes=VMEM_LIMIT),
    )(*ins)


def exchange(value, axis, step):
    count = lax.axis_size(axis)
    return lax.ppermute(value, axis, [(k, k ^ step) for k in range(count)])


def packers():
    per, taken, sent = 2 * CAP, SENT_ROWS, BACK_ROWS
    pack = np.zeros((11, CHIPS, per, CHIPS, taken), np.float32)
    unpack = np.zeros((13, CHIPS, sent, CHIPS * per + 16), np.float32)
    for j in range(CHIPS):
        for k in range(per):
            pack[10, j, k, j, k] = 1.0
            if k < 8:
                unpack[0, j, k, j * per + k] = 1.0
            for kind in range(2):
                if k < 8:
                    pack[5 * kind, j, k, j, 8 * kind + k] = 1.0
                else:
                    for m in range(4):
                        pack[5 * kind + 1 + m, j, k, j, 4 * (k - 8 + 2 * kind) + m] = 1.0
        for i in range(6):
            source = j * per + 8 + i if i < 2 else CHIPS * per + i - 2
            for m in range(4):
                r, c = (4 * i + m) // 3, (4 * i + m) % 3
                unpack[1 + 4 * c + m, j, r, source] = 1.0
    pack = pack.reshape(11 * CHIPS * per, CHIPS * taken)
    unpack = unpack.reshape(13 * CHIPS * sent, CHIPS * per + 16)
    return jnp.asarray(pack, BF), jnp.asarray(unpack, BF)


def shards(stash, out_grad, router_weight, gate_weight, up_weight, down_weight, expert_ids):
    experts, ways = router_weight.shape[0], lax.axis_size("t")
    tokens, width = stash.shape[1], stash.shape[2]
    hidden = gate_weight.shape[0]
    share = hidden // ways
    router_tall = jnp.pad(router_weight, ((0, 128 - experts), (0, 0)))
    packer, unpacker = packers()
    slots = 2 * CHIPS * CAP
    height = slots + 8

    places = 2 * CHIPS
    x_other = lax.ppermute(stash[0], ("p", "c"), [(k, places - 1 - k) for k in range(places)])
    id_columns = jnp.pad(jnp.concatenate([expert_ids[0]] * 2, 0).astype(BF), ((0, 0), (0, 126)))
    block = jnp.concatenate([jnp.concatenate([x_other, out_grad[0]], 0), id_columns], 1)
    (ready,) = call(
        ready_kernel, [x_other, gate_weight, up_weight, down_weight], [((tokens, 128), F32)], 1000
    )
    chosen, own_block = call(
        functools.partial(pick_kernel, width),
        [block, exchange(block, "h", 1), ready],
        [((CHIPS, SENT_ROWS, width + width // 4 + 128), BF), ((2 * tokens, width + 128), BF)],
        8 * width * 32 * SENT_ROWS,
    )
    near = lax.all_to_all(chosen, "p", 0, 0).reshape(CHIPS * SENT_ROWS, -1)
    far = exchange(near, "c", 1)

    halves = []
    for index, block in enumerate((near, far)):
        if index == 1:
            block, _ = lax.optimization_barrier((block, halves[0][0]))
        steps = (1, 2, 3) if index else (3,)
        types = (BF, F32, BF) if index else (BF,)
        *sends, mine, taken = call(
            functools.partial(project_kernel, width, share, index == 0, steps),
            [block, gate_weight, up_weight, down_weight, router_tall, packer, own_block],
            [((height, 3 * share), dtype) for dtype in types]
            + [((height, 3 * share + 128), F32), ((2 * slots, width), BF)],
            2 * slots * width * (3 * share * len(steps) + 4 * slots),
            [pltpu.VMEM((8, 3 * share), F32)],
        )
        if index == 0:
            later = call(
                functools.partial(rest_kernel, share),
                [mine, taken, gate_weight, up_weight, down_weight],
                [((height, 3 * share), BF)] * 2 + [((height, 3 * share + 128), F32)],
                2 * slots * width * 9 * share,
            )
            sends, mine = [later[1], later[0], sends[0]], later[2]
        if index == 0:
            got = [exchange(sends[step - 1], "t", step) for step in (3, 2, 1)]
        else:
            passed = exchange(sends[2], "t", 1)
            sends[1], halves[0][1][0] = lax.optimization_barrier((sends[1], halves[0][1][0]))
            (relayed,) = call(
                functools.partial(relay_kernel, slots, share),
                [sends[1], passed],
                [((height, 3 * share), BF)],
                slots * share * 6,
            )
            beside, relayed = lax.optimization_barrier((sends[0], relayed))
            got = [exchange(relayed, "t", 2), exchange(beside, "t", 1)]
        halves.append((mine, got, taken))
    gradients = []
    for index, (mine, got, taken) in enumerate(halves):
        packed, weight, local, losses = call(
            functools.partial(act_kernel, width, slots, share, experts, index == 0),
            [own_block, mine, *got],
            [((height, 3 * share), BF), ((slots, 128), F32), ((16, 128), F32), ((1, 2), F32)],
            slots * share * 40,
        )
        packed_one = packed
        if index == 1:
            packed_one, gradients[0][0][1] = lax.optimization_barrier((packed, gradients[0][0][1]))
        pieces = [packed, exchange(packed_one, "t", 1), exchange(packed, "t", 2)]
        pieces.append(exchange(pieces[2], "t", 1))
        gradients.append((pieces, weight, local, losses))
    _, _, local, losses = gradients[0]

    pieces, weight, _, _ = gradients[0]
    kept, router_near = call(
        functools.partial(near_kernel, width, share),
        [*pieces, gate_weight, up_weight, router_tall, weight, halves[0][2], local, own_block],
        [((slots, width), F32), ((8, width), F32)],
        2 * slots * width * 2 * hidden,
    )
    pieces, weight, _, _ = gradients[1]
    sent, router_part = call(
        functools.partial(far_kernel, share),
        [*pieces, gate_weight, up_weight, router_tall, weight, halves[1][2], router_near],
        [((slots + 16, width), BF), ((8, width), F32)],
        2 * slots * width * 2 * hidden,
    )
    got = exchange(sent, "c", 1)
    (pair,) = call(
        functools.partial(pair_kernel, width),
        [kept, got, router_part, unpacker],
        [((CHIPS * BACK_ROWS, width + 3 * (width // 4)), BF)],
        2 * slots * slots * width,
    )
    got = lax.all_to_all(pair.reshape(CHIPS, BACK_ROWS, -1), "p", 0, 0)
    own_rows, router_part, sent = call(
        functools.partial(group_kernel, width),
        [got],
        [((16, width), F32), ((8, width), F32), ((16, width), BF)],
        slots * width * 2,
    )
    gate_grad, up_grad, down_grad = call(
        functools.partial(weight_kernel, slots, share),
        [*gradients[0][0], halves[0][2], *gradients[1][0], halves[1][2]],
        [((hidden, width), BF)] * 3,
        4 * slots * width * hidden * 3,
        [pltpu.VMEM((3, ways, share, width), BF), pltpu.SemaphoreType.DMA((3, ways))],
        pl.BlockSpec(memory_space=pl.ANY),
    )
    (base,) = call(
        functools.partial(base_kernel, width),
        [own_rows, own_block, local, router_tall],
        [((tokens, width), F32)],
        tokens * width * 30,
    )
    in_grad, router_grad = call(
        functools.partial(final_kernel, width, experts),
        [base, router_part, exchange(sent, "h", 1), own_block],
        [((tokens, width), BF), ((experts, width), F32)],
        tokens * width * 50,
    )
    return in_grad[None], gate_grad, up_grad, down_grad, router_grad, losses


def solution(mesh):
    ways = mesh.devices.shape[1]
    fine = Mesh(mesh.devices.reshape(2, CHIPS, 2, ways), ("h", "p", "c", "t"))
    section = ("h", "p", "c")
    in_specs = (
        P(section, None, "t"),
        P(section, None, "t"),
        P(None, "t"),
        P(section, "t"),
        P(section, "t"),
        P(section, "t"),
        P(section, None, None),
    )
    out_specs = (
        P(section, None, "t"),
        P(section, "t"),
        P(section, "t"),
        P(section, "t"),
        P(None, "t"),
        P(section, None),
    )
    return jax.shard_map(shards, mesh=fine, in_specs=in_specs, out_specs=out_specs, check_vma=False)
```
